32 devices in a mesh: groups: 2 (over x), row: 16 (over z, y, core).
Axes of the slice: x: 2, y: 2, z: 4, core: 2. Of those that a mesh axis runs over, the one named last changes fastest.
Arguments:
- features: bfloat16 [32768, 256], P(('groups', 'row')), parts along dimension 0, may hold values from -6 to 6
- weight: bfloat16 [256, 256], replicated, may hold values from -0.375 to 0.375
- root_weight: bfloat16 [256, 256], replicated, may hold values from -0.375 to 0.375
- block_tiles: bfloat16 [6144, 128, 128], P(('groups', 'row')), parts along dimension 0, may hold values from -0.109375 to 0.109375
- tile_rows: int32 [6144], P(('groups', 'row')), parts along dimension 0, may hold values from 0 to 7, as said below
- tile_cols: int32 [6144], P(('groups', 'row')), parts along dimension 0, may hold values from 0 to 127, as said below
- tile_count: int32 [32], P(('groups', 'row')), parts along dimension 0, may hold values from 48 to 192, as said below
- cotangent: bfloat16 [32768, 256], P(('groups', 'row')), parts along dimension 0, may hold values from -6 to 6
Outputs:
- layer_out: bfloat16 [32768, 256], P(('groups', 'row')), parts along dimension 0
- grad_features: bfloat16 [32768, 256], P(('groups', 'row')), parts along dimension 0
- grad_weight: float32 [512, 256], P('groups'), parts along dimension 0
- grad_root: float32 [512, 256], P('groups'), parts along dimension 0
The draws below stay inside these ranges and needn't reach their ends.
There are 2 independent parts, one for each index of `groups`. The reference program is written for one: setup_inputs(seed, part) draws one part's arguments, and reference() takes and returns one part's arrays. A program takes and returns all parts, laid end to end along the dimension named above; an argument that names none is the same for every part. Nothing has to cross between parts.
Inputs may be any that keep to these rules, and one draw needn't show every extreme that they name: `tile_rows`: the row block of a slot within its stripe of 8 blocks; stripe s owns slots s * 192 to (s + 1) * 192 - 1. `tile_cols`: a slot of stripe s names a column block from (s - 2) * 8 to (s + 3) * 8 - 1 that lies in the graph; within a stripe no pair of row block and column block appears twice, live or not. The live slots of each stripe are its first tile_count slots; some stripe has all 192 live.
All inputs are finite; a program needn't handle non-finite values.
Results may differ from the reference program's by a relative error of at most 0.0055.
Values may be sent and summed in bfloat16 or wider, within the bound.
No kernel may reach another device: no remote copies, remote signals or barrier semaphores. Data moves between devices by JAX's collectives and lax.ppermute only.
A program may use at most 128 MiB of HBM per device.

```python
import math
import jax
import jax.numpy as jnp
from jax import lax

FEAT = 256
BLOCK = 128
REACH = 2
BLK_DEV = 8
SLOTS = 192
STRIPES = 16
NODES = 16384


def tile_layout(key):
    key = jax.random.fold_in(key, 11)
    window_width = (2 * REACH + 1) * BLK_DEV
    position = jnp.arange(BLK_DEV * window_width, dtype=jnp.int32)
    stripes = jnp.arange(STRIPES, dtype=jnp.int32)[:, None]
    columns = (stripes - REACH) * BLK_DEV + position[None, :] % window_width
    inside = (columns >= 0) & (columns < STRIPES * BLK_DEV)
    first_row = position[None, :] < window_width
    forced = first_row & ((columns == 0) | (columns == STRIPES * BLK_DEV - 1))
    random_keys = jax.random.randint(key, (STRIPES, BLK_DEV * window_width), 0, 2 ** 17, dtype=jnp.int32)
    base = jnp.where(inside, jnp.int32(2 ** 28), jnp.int32(2 ** 30))
    base = jnp.where(forced, jnp.int32(0), base)
    sort_keys = base + random_keys * 2048 + position[None, :]
    chosen = jnp.argsort(sort_keys, axis=1, stable=True)[:, :SLOTS].astype(jnp.int32)
    row_blocks = (chosen // window_width).astype(jnp.int32)
    col_blocks = jnp.take_along_axis(columns, chosen, axis=1).astype(jnp.int32)
    return (row_blocks.reshape(-1), col_blocks.reshape(-1))


def draw_tile_rows(key, part):
    row_blocks, col_blocks = tile_layout(key)
    return row_blocks


def draw_tile_cols(key, part):
    row_blocks, col_blocks = tile_layout(key)
    return col_blocks


def draw_tile_count(key, part):
    key = jax.random.fold_in(key, 5)
    count_key, full_key = jax.random.split(key)
    counts = jax.random.randint(count_key, (STRIPES,), SLOTS // 4, SLOTS + 1, dtype=jnp.int32)
    full_stripe = jax.random.randint(full_key, (), 0, STRIPES, dtype=jnp.int32)
    return jnp.where(jnp.arange(STRIPES, dtype=jnp.int32) == full_stripe, jnp.int32(SLOTS), counts).astype(jnp.int32)


def block_scale(stream_key, dims, cuts, smallest, high):
    loudness, own = 1.0, jax.random.fold_in(stream_key, 6)
    for axis_at, shards_of in cuts:
        steps = jnp.exp(jax.random.uniform(jax.random.fold_in(own, axis_at), (shards_of,), jnp.float32, smallest / len(cuts), high / len(cuts)))
        loudness = loudness * jnp.repeat(steps, dims[axis_at] // shards_of).reshape([-1 if axis == axis_at else 1 for axis in range(len(dims))])
    return loudness


def noise(key, dims, spread, bound, shards=(), held_as=jnp.bfloat16):
    drawn = jax.random.normal(key, dims, jnp.float32) * spread
    if len(shards) > 0:
        drawn = block_scale(key, dims, shards, -0.22, 0.18) * drawn
    return jnp.clip(drawn, min=-bound, max=bound).astype(held_as)


def setup_inputs(seed: int = 0, part: int = 0) -> dict:
    splits = jax.random.split(jax.random.key(seed), 9)
    part_keys = jax.random.split(jax.random.fold_in(splits[8], part), 9)
    features = noise(part_keys[0], (NODES, FEAT), 1.0, 6.0, ((0, 16),))
    weight = noise(splits[1], (FEAT, FEAT), FEAT ** -0.5, 0.375)
    root_weight = noise(splits[2], (FEAT, FEAT), FEAT ** -0.5, 0.375)
    block_tiles = noise(part_keys[3], (STRIPES * SLOTS, BLOCK, BLOCK), (SLOTS * BLOCK // BLK_DEV) ** -0.5, 0.109375, ((0, 16),))
    tile_rows = draw_tile_rows(jax.random.fold_in(jax.random.fold_in(splits[8], part), 71), part)
    tile_cols = draw_tile_cols(jax.random.fold_in(jax.random.fold_in(splits[8], part), 71), part)
    tile_count = draw_tile_count(jax.random.fold_in(jax.random.fold_in(splits[8], part), 71), part)
    cotangent = noise(part_keys[7], (NODES, FEAT), 1.0, 6.0, ((0, 16),))
    return {"features": features, "weight": weight, "root_weight": root_weight, "block_tiles": block_tiles, "tile_rows": tile_rows, "tile_cols": tile_cols, "tile_count": tile_count, "cotangent": cotangent}


def silu_slope(pre_act):
    sigmoid_pre = jax.nn.sigmoid(pre_act)
    return sigmoid_pre * (1.0 + pre_act * (1.0 - sigmoid_pre))

def reference(features, weight, root_weight, block_tiles, tile_rows, tile_cols, tile_count, cotangent):
    node_count = features.shape[0]
    block_count = node_count // BLOCK
    projected = jnp.dot(features, weight, preferred_element_type=jnp.float32).astype(jnp.bfloat16)
    root_term = jnp.dot(features, root_weight, preferred_element_type=jnp.float32)
    stripe_tiles = block_tiles.reshape(STRIPES, SLOTS, BLOCK, BLOCK)
    stripe_rows = tile_rows.reshape(STRIPES, SLOTS)
    stripe_cols = tile_cols.reshape(STRIPES, SLOTS)
    slot_ids = jnp.arange(SLOTS, dtype=jnp.int32)
    proj_blocks = projected.reshape(block_count, BLOCK, FEAT)

    def forward_stripe(stripe_number):
        live_mask = (slot_ids < tile_count[stripe_number]).astype(jnp.float32)
        sources = proj_blocks[stripe_cols[stripe_number]].astype(jnp.float32)
        products = jnp.einsum('tij,tjf->tif', stripe_tiles[stripe_number].astype(jnp.float32), sources)
        products = products * live_mask[:, None, None]
        return jnp.zeros((BLK_DEV, BLOCK, FEAT), jnp.float32).at[stripe_rows[stripe_number]].add(products)
    aggregated = lax.map(forward_stripe, jnp.arange(STRIPES, dtype=jnp.int32)).reshape(node_count, FEAT)
    pre_act = aggregated + root_term
    layer_out = jax.nn.silu(pre_act).astype(jnp.bfloat16)
    grad_pre = (cotangent.astype(jnp.float32) * silu_slope(pre_act)).astype(jnp.bfloat16)
    grad_blocks = grad_pre.reshape(block_count, BLOCK, FEAT)

    def backward_stripe(column_sums, stripe_number):
        live_mask = (slot_ids < tile_count[stripe_number]).astype(jnp.float32)
        row_index = (stripe_number * BLK_DEV + stripe_rows[stripe_number]).astype(jnp.int32)
        sources = grad_blocks[row_index].astype(jnp.float32)
        products = jnp.einsum('tji,tjf->tif', stripe_tiles[stripe_number].astype(jnp.float32), sources)
        products = products * live_mask[:, None, None]
        return (column_sums.at[stripe_cols[stripe_number]].add(products), None)
    column_sums, _ = lax.scan(backward_stripe, jnp.zeros((block_count, BLOCK, FEAT), jnp.float32), jnp.arange(STRIPES, dtype=jnp.int32))
    grad_proj = column_sums.reshape(node_count, FEAT).astype(jnp.bfloat16)
    grad_scale = 1.0 / math.sqrt(node_count)
    grad_weight = jnp.dot(features.T, grad_proj, preferred_element_type=jnp.float32) * grad_scale
    grad_root = jnp.dot(features.T, grad_pre, preferred_element_type=jnp.float32) * grad_scale
    grad_features = jnp.dot(grad_proj, weight.T, preferred_element_type=jnp.float32) + jnp.dot(grad_pre, root_weight.T, preferred_element_type=jnp.float32)
    return (layer_out, grad_features.astype(jnp.bfloat16), grad_weight, grad_root)
```

```python
import functools
import math

import jax
import jax.numpy as jnp
from jax import lax
from jax.experimental import pallas as pl
from jax.experimental.pallas import tpu as pltpu
from jax.sharding import PartitionSpec as P

REACH = 2
F32, BF16 = jnp.float32, jnp.bfloat16

OWN, OWN_X, SIDE, SIDE_X, PLANE, PLANE_X = range(6)
PARTS = 6


def vmem_spec():
    return pl.BlockSpec(memory_space=pltpu.VMEM)


def smem_spec():
    return pl.BlockSpec(memory_space=pltpu.SMEM)


def in_vmem(array):
    return pltpu.with_memory_space_constraint(array, pltpu.VMEM)


def kernel_call(kernel, name, outs, args, flops, bytes_accessed=1 << 20):
    return pl.pallas_call(
        kernel,
        out_shape=[pltpu.VMEM(shape, dtype) for shape, dtype in outs],
        in_specs=[vmem_spec()] * len(args),
        out_specs=[vmem_spec()] * len(outs),
        compiler_params=pltpu.CompilerParams(vmem_limit_bytes=12 << 20),
        cost_estimate=pl.CostEstimate(flops=flops, bytes_accessed=bytes_accessed, transcendentals=0),
        name=name,
    )(*[in_vmem(a) for a in args])


def flip_core(array, count):
    return lax.ppermute(array, "row", [(i, i ^ 1) for i in range(count)])


def flip_side(array, count):
    return lax.ppermute(array, "row", [(i, i ^ 2) for i in range(count)])


def over_planes(array, count, back):
    step = [(i, i + 4) for i in range(count) if i % 4 < 2 and i + 4 < count]
    step += [(i, i - 4) for i in range(count) if i % 4 >= 2 and i >= 4]
    return lax.ppermute(array, "row", [(b, a) for a, b in step] if back else step)


def dense_kernel(stripe_ref, rows_ref, cols_ref, count_ref, tiles_ref, a_ref, sem):
    block = tiles_ref.shape[1]
    width = a_ref.shape[1]
    blocks = width // block
    stripe = stripe_ref[0]
    core, side = stripe & 1, (stripe >> 1) & 1
    first = (stripe >> 1) * (2 * blocks)
    live = count_ref[0]

    def clear(i, carry):
        for part in range(PARTS):
            a_ref[part, pl.ds(pl.multiple_of(i * 64, 64), 64), :] = jnp.zeros((64, width), BF16)
        return carry

    def placed(slot):
        away = cols_ref[slot] - first + 2 * blocks
        chip = away // (2 * blocks)
        within = away - chip * (2 * blocks)
        other = within // blocks
        column = within - other * blocks
        near = jnp.where(side == 0, 2, 0)
        part = jnp.where(chip == 1, OWN, jnp.where(chip == near, SIDE, PLANE)) + (other ^ core)
        target = a_ref.at[
            part,
            pl.ds(pl.multiple_of(rows_ref[slot] * block, block), block),
            pl.ds(pl.multiple_of(column * block, block), block),
        ]
        return pltpu.make_async_copy(tiles_ref.at[slot], target, sem)

    def start(slot, carry):
        placed(slot).start()
        return carry

    def finish(slot, carry):
        placed(slot).wait()
        return carry

    lax.fori_loop(0, width // 64, clear, 0)
    lax.fori_loop(0, live, start, 0)
    lax.fori_loop(0, live, finish, 0)


def dense_adjacency(stripe, tile_rows, tile_cols, tile_count, block_tiles, width):
    return pl.pallas_call(
        dense_kernel,
        out_shape=pltpu.VMEM((PARTS, width, width), BF16),
        in_specs=[smem_spec()] * 4 + [pl.BlockSpec(memory_space=pl.ANY)],
        out_specs=vmem_spec(),
        scratch_shapes=[pltpu.SemaphoreType.DMA],
        compiler_params=pltpu.CompilerParams(vmem_limit_bytes=12 << 20),
        cost_estimate=pl.CostEstimate(flops=0, bytes_accessed=20 << 20, transcendentals=0),
        name="dense_adjacency",
    )(stripe, tile_rows, tile_cols, tile_count, block_tiles)


def dot(a, b):
    return jnp.dot(a, b, preferred_element_type=F32)


def dot_nt(a, b):
    return lax.dot_general(a, b, (((1,), (1,)), ((), ())), preferred_element_type=F32)


def gather_kernel(terms, started, *refs):
    a_ref, out_ref = refs[0], refs[-1]
    sources = refs[1:-1]
    total = sources[-1][...] if started else None
    for (part, low), source in zip(terms, sources):
        product = dot(a_ref[part, :, low : low + source.shape[0]], source[...])
        total = product if total is None else total + product
    out_ref[...] = total


def gathered(dense, terms, sources, total, name):
    rows, width = dense.shape[1], sources[0].shape[1]
    args = [dense, *sources] + ([] if total is None else [total])
    flops = sum(2 * rows * s.shape[0] * width for s in sources)
    return kernel_call(
        functools.partial(gather_kernel, terms, total is not None), name, [((rows, width), F32)], args, flops
    )[0]


def middle_kernel(
    half, a_ref, last_ref, total_ref, x_ref, w_ref, r_ref, cot_ref,
    out_ref, grad_ref, ax_ref, ht_ref, low_ref, high_ref,
):
    rows = x_ref.shape[0]
    step = 256
    for at in range(0, rows, step):
        here = slice(at, at + step)
        ax = total_ref[here, :] + dot(a_ref[PLANE_X, here, half:], last_ref[...])
        ax = ax.astype(BF16)
        ax_ref[here, :] = ax
        pre = dot(ax, w_ref[...]) + dot(x_ref[here, :], r_ref[...])
        gate = jax.nn.sigmoid(pre)
        out_ref[here, :] = (pre * gate).astype(BF16)
        grad = (cot_ref[here, :].astype(F32) * (gate * (1.0 + pre * (1.0 - gate)))).astype(BF16)
        grad_ref[here, :] = grad
        ht_ref[:, here] = dot_nt(w_ref[...], grad).astype(BF16)
    low_ref[...] = dot(ht_ref[...], a_ref[PLANE_X, :, :half]).T.astype(BF16)
    high_ref[...] = dot(ht_ref[...], a_ref[PLANE_X, :, half:]).T.astype(BF16)


def spread_kernel(part, half, a_ref, ht_ref, low_ref, high_ref):
    low_ref[...] = dot(ht_ref[...], a_ref[part, :, :half]).T.astype(low_ref.dtype)
    high_ref[...] = dot(ht_ref[...], a_ref[part, :, half:]).T.astype(high_ref.dtype)


def spread(dense, ht, part, half, dtype, name):
    rows, width = dense.shape[1], ht.shape[0]
    return kernel_call(
        functools.partial(spread_kernel, part, half),
        name,
        [((half, width), dtype), ((rows - half, width), dtype)],
        [dense, ht],
        2 * rows * rows * width,
    )


def own_kernel(half, a_ref, ht_ref, grad_ref, r_ref, low_ref, high_ref):
    for out, here in ((low_ref, slice(0, half)), (high_ref, slice(half, None))):
        out[...] = dot(ht_ref[...], a_ref[OWN, :, here]).T + dot_nt(grad_ref[here, :], r_ref[...])


def final_kernel(half, own0_ref, own1_ref, x0_ref, x1_ref, in0_ref, in1_ref, out_ref):
    out_ref[:half, :] = (own0_ref[...] + x0_ref[...].astype(F32) + in0_ref[...].astype(F32)).astype(BF16)
    out_ref[half:, :] = (own1_ref[...] + x1_ref[...].astype(F32) + in1_ref[...].astype(F32)).astype(BF16)


def added(a, b, name):
    return (a.astype(F32) + b.astype(F32)).astype(BF16)


def weight_sums(local_weight, local_root, core, side, count):
    kept = jnp.where(core == 0, local_weight, local_root)
    kept = kept + flip_core(jnp.where(core == 0, local_root, local_weight), count)
    half = kept.shape[0] // 2
    top, bottom = kept[:half], kept[half:]
    part = jnp.where(side == 0, top, bottom) + flip_side(jnp.where(side == 0, bottom, top), count)
    hop = 4
    while hop < count:
        part = part + lax.ppermute(part, "row", [(i, i ^ hop) for i in range(count)])
        hop *= 2
    other = flip_side(part, count)
    kept = jnp.concatenate([jnp.where(side == 0, part, other), jnp.where(side == 0, other, part)], axis=0)
    other = flip_core(kept, count)
    return jnp.where(core == 0, kept, other), jnp.where(core == 0, other, kept)


def body(features, weight, root_weight, block_tiles, tile_rows, tile_cols, tile_count, cotangent):
    count = lax.axis_size("row")
    rows, width = features.shape
    half = rows // 2
    index = lax.axis_index("row").astype(jnp.int32)
    core, side = index & 1, (index >> 1) & 1

    low, high = features[:half], features[half:]
    side_low = flip_side(low, count)
    side_high = flip_side(high, count)
    own_x = flip_core(features, count)
    plane_low = over_planes(side_low, count, False)
    plane_high = over_planes(side_high, count, False)
    side_x_low = flip_core(side_low, count)
    side_x_high = flip_core(side_high, count)
    plane_x_low = flip_core(plane_low, count)
    plane_x_high = flip_core(plane_high, count)

    dense = dense_adjacency(index.reshape(1), tile_rows, tile_cols, tile_count, block_tiles, rows)
    total = gathered(dense, [(OWN, 0), (OWN_X, 0)], [features, own_x], None, "gather_own")
    total = gathered(
        dense,
        [(SIDE, 0), (SIDE, half), (SIDE_X, 0), (SIDE_X, half)],
        [side_low, side_high, side_x_low, side_x_high],
        total,
        "gather_side",
    )
    total = gathered(
        dense,
        [(PLANE, 0), (PLANE_X, 0), (PLANE, half)],
        [plane_low, plane_x_low, plane_high],
        total,
        "gather_plane",
    )
    layer_out, grad_pre, gathered_x, ht, px_low, px_high = kernel_call(
        functools.partial(middle_kernel, half),
        "middle",
        [
            ((rows, width), BF16),
            ((rows, width), BF16),
            ((rows, width), BF16),
            ((width, rows), BF16),
            ((half, width), BF16),
            ((rows - half, width), BF16),
        ],
        [dense, plane_x_high, total, features, weight, root_weight, cotangent],
        3 * 2 * rows * rows * width,
    )

    px_low, px_high = flip_core(px_low, count), flip_core(px_high, count)
    p_low, p_high = spread(dense, ht, PLANE, half, BF16, "spread_plane")
    far_low = over_planes(added(p_low, px_low, "low"), count, True)
    far_high = over_planes(added(p_high, px_high, "high"), count, True)
    sx_low, sx_high = spread(dense, ht, SIDE_X, half, BF16, "spread_side_x")
    sx_low, sx_high = flip_core(sx_low, count), flip_core(sx_high, count)
    s_low, s_high = spread(dense, ht, SIDE, half, F32, "spread_side")
    s_low, s_high = s_low + sx_low.astype(F32), s_high + sx_high.astype(F32)
    ox_low, ox_high = spread(dense, ht, OWN_X, half, BF16, "spread_own_x")
    ox_low, ox_high = flip_core(ox_low, count), flip_core(ox_high, count)
    own_low, own_high = kernel_call(
        functools.partial(own_kernel, half),
        "spread_own",
        [((half, width), F32), ((rows - half, width), F32)],
        [dense, ht, grad_pre, root_weight],
        3 * rows * rows * width,
    )
    in_low = flip_side(added(s_low, far_low, "low"), count)
    in_high = flip_side(added(s_high, far_high, "high"), count)

    grad_scale = 1.0 / math.sqrt(count * rows)
    local_weight = jnp.einsum("nf,ng->fg", gathered_x, grad_pre, preferred_element_type=F32)
    local_root = jnp.einsum("nf,ng->fg", features, grad_pre, preferred_element_type=F32)
    total_weight, total_root = weight_sums(local_weight, local_root, core, side, count)

    grad_features = kernel_call(
        functools.partial(final_kernel, half),
        "final",
        [((rows, width), BF16)],
        [own_low, own_high, ox_low, ox_high, in_low, in_high],
        rows * width * 4,
    )[0]
    return layer_out, grad_features, total_weight * grad_scale, total_root * grad_scale


def solution(mesh):
    placed = (
        P(("groups", "row"), None),
        P(),
        P(),
        P(("groups", "row"), None, None),
        P(("groups", "row")),
        P(("groups", "row")),
        P(("groups", "row")),
        P(("groups", "row"), None),
    )
    return jax.shard_map(
        body,
        mesh=mesh,
        in_specs=placed,
        out_specs=(
            P(("groups", "row"), None),
            P(("groups", "row"), None),
            P("groups", None),
            P("groups", None),
        ),
        check_vma=False,
    )
```

```python
import functools
import math

import jax
import jax.numpy as jnp
from jax import lax
from jax.experimental import pallas as pl
from jax.experimental.pallas import tpu as pltpu
from jax.sharding import PartitionSpec as P

REACH = 2
F32, BF16 = jnp.float32, jnp.bfloat16

OWN, OWN_X, SIDE, SIDE_X, PLANE, PLANE_X = range(6)
PARTS = 6
LIMIT = 4 << 20
CUT = 128
COST = pl.CostEstimate(flops=0, bytes_accessed=0, transcendentals=0)
FORWARD = 8
BACKWARD = 8


def vmem_spec():
    return pl.BlockSpec(memory_space=pltpu.VMEM)


def after(array, *others):
    return lax.optimization_barrier((array, *others))[0]


def smem_spec():
    return pl.BlockSpec(memory_space=pltpu.SMEM)


def hbm_spec():
    return pl.BlockSpec(memory_space=pltpu.HBM)


def in_vmem(array):
    return pltpu.with_memory_space_constraint(array, pltpu.VMEM)


def in_hbm(array):
    return pltpu.with_memory_space_constraint(array, pltpu.HBM)


def kernel_call(kernel, name, outs, args):
    return pl.pallas_call(
        kernel,
        out_shape=[pltpu.VMEM(shape, dtype) for shape, dtype in outs],
        in_specs=[vmem_spec()] * len(args),
        out_specs=[vmem_spec()] * len(outs),
        compiler_params=pltpu.CompilerParams(vmem_limit_bytes=LIMIT),
        cost_estimate=COST,
        name=name,
    )(*[in_vmem(a) for a in args])


def flip_core(array, count):
    return lax.ppermute(array, "row", [(i, i ^ 1) for i in range(count)])


def flip_side(array, count):
    return lax.ppermute(array, "row", [(i, i ^ 2) for i in range(count)])


def over_planes(array, count, back, ends):
    step = [(i, i + 4) for i in range(count) if i % 4 < 2 and i + 4 < count]
    step += [(i, i - 4) for i in range(count) if i % 4 >= 2 and i >= 4]
    if ends:
        step += [(count - 4, count - 2), (count - 3, count - 1), (2, 0), (3, 1)]
    return lax.ppermute(array, "row", [(b, a) for a, b in step] if back else step)


def past_side(array, count, back):
    step = [(i, (i ^ 2) + 4) for i in range(count) if i % 4 >= 2 and i + 4 < count]
    step += [(i, (i ^ 2) - 4) for i in range(count) if i % 4 < 2 and i >= 4]
    return lax.ppermute(array, "row", [(b, a) for a, b in step] if back else step)


def dense_kernel(count_ref, rows_hbm, cols_hbm, tiles_ref, a_ref, rows_ref, cols_ref, sem, index_sems):
    block = tiles_ref.shape[1]
    width = a_ref.shape[1]
    blocks = width // block
    fetches = [
        pltpu.make_async_copy(src, dst, index_sems.at[i])
        for i, (src, dst) in enumerate(((rows_hbm, rows_ref), (cols_hbm, cols_ref)))
    ]
    for fetch in fetches:
        fetch.start()
    stripe = lax.axis_index("row")
    core, side = stripe & 1, (stripe >> 1) & 1
    first = (stripe >> 1) * (2 * blocks)

    def clear(i, carry):
        for part in range(PARTS):
            a_ref[part, pl.ds(pl.multiple_of(i * 64, 64), 64), :] = jnp.zeros((64, width), BF16)
        return carry

    def placed(slot):
        away = cols_ref[slot] - first + 2 * blocks
        chip = away // (2 * blocks)
        within = away - chip * (2 * blocks)
        other = within // blocks
        column = within - other * blocks
        near = jnp.where(side == 0, 2, 0)
        part = jnp.where(chip == 1, OWN, jnp.where(chip == near, SIDE, PLANE)) + (other ^ core)
        target = a_ref.at[
            part,
            pl.ds(pl.multiple_of(rows_ref[slot] * block, block), block),
            pl.ds(pl.multiple_of(column * block, block), block),
        ]
        return pltpu.make_async_copy(tiles_ref.at[slot], target, sem)

    def start(slot, carry):
        placed(slot).start()
        return carry

    def finish(slot, carry):
        placed(slot).wait()
        return carry

    lax.fori_loop(0, width // 64, clear, 0)
    for fetch in fetches:
        fetch.wait()
    live = count_ref[0]
    lax.fori_loop(0, live, start, 0)
    lax.fori_loop(0, live, finish, 0)


def dense_adjacency(tile_rows, tile_cols, tile_count, block_tiles, width):
    slots = tile_rows.shape[0]
    return pl.pallas_call(
        dense_kernel,
        out_shape=pltpu.VMEM((PARTS, width, width), BF16),
        in_specs=[smem_spec()] + [hbm_spec()] * 3,
        out_specs=vmem_spec(),
        scratch_shapes=[
            pltpu.SMEM((slots,), jnp.int32),
            pltpu.SMEM((slots,), jnp.int32),
            pltpu.SemaphoreType.DMA,
            pltpu.SemaphoreType.DMA((2,)),
        ],
        compiler_params=pltpu.CompilerParams(vmem_limit_bytes=LIMIT),
        cost_estimate=COST,
        name="dense_adjacency",
    )(tile_count, *[in_hbm(a) for a in (tile_rows, tile_cols, block_tiles)])


def dot(a, b):
    return jnp.dot(a, b, preferred_element_type=F32)


def dot_nt(a, b):
    return lax.dot_general(a, b, (((1,), (1,)), ((), ())), preferred_element_type=F32)


def dot_tn(a, b):
    return lax.dot_general(a, b, (((0,), (0,)), ((), ())), preferred_element_type=F32)


def gather_kernel(terms, started, *refs):
    a_ref, out_ref = refs[0], refs[-1]
    sources = refs[1:-1]
    total = sources[-1][...] if started else None
    for (part, low), source in zip(terms, sources):
        product = dot(a_ref[part, :, low : low + source.shape[0]], source[...])
        total = product if total is None else total + product
    out_ref[...] = total


def gathered(dense, terms, sources, total, name):
    rows, width = dense.shape[1], sources[0].shape[1]
    args = [dense, *sources] + ([] if total is None else [total])
    return kernel_call(
        functools.partial(gather_kernel, terms, total is not None), name, [((rows, width), F32)], args
    )[0]


def cut_kernel(at, src_ref, out_ref, sems):
    copies = []
    rows = out_ref.shape[0]
    for i, low in enumerate(range(0, rows, CUT)):
        size = min(CUT, rows - low)
        copies.append(
            pltpu.make_async_copy(src_ref.at[pl.ds(at + low, size)], out_ref.at[pl.ds(low, size)], sems.at[i])
        )
    for copy in copies:
        copy.start()
    for copy in copies:
        copy.wait()


def cut(array, at, end):
    return pl.pallas_call(
        functools.partial(cut_kernel, at),
        out_shape=pltpu.VMEM((end - at, array.shape[1]), array.dtype),
        in_specs=[hbm_spec()],
        out_specs=vmem_spec(),
        scratch_shapes=[pltpu.SemaphoreType.DMA((pl.cdiv(end - at, CUT),))],
        compiler_params=pltpu.CompilerParams(vmem_limit_bytes=LIMIT),
        cost_estimate=COST,
        name="cut",
    )(in_hbm(array))


def middle_kernel(terms, end, a_ref, total_ref, x_ref, w_ref, r_ref, cot_ref, *refs):
    last_refs, refs = refs[: len(terms)], refs[len(terms) :]
    out_hbm, grad_ref, ax_ref, ht_ref, px_ref, out_ref, sems = refs
    rows = x_ref.shape[0]
    step = rows // sems.shape[0]
    copies = []
    for i in range(sems.shape[0]):
        here = slice(i * step, (i + 1) * step)
        ax = total_ref[here, :]
        for (part, low, high), last_ref in zip(terms, last_refs):
            ax = ax + dot(a_ref[part, here, low:high], last_ref[...])
        ax = ax.astype(BF16)
        ax_ref[here, :] = ax
        pre = dot(ax, w_ref[...]) + dot(x_ref[here, :], r_ref[...])
        gate = jax.nn.sigmoid(pre)
        out_ref[here, :] = (pre * gate).astype(BF16)
        copies.append(
            pltpu.make_async_copy(
                out_ref.at[pl.ds(i * step, step)], out_hbm.at[pl.ds(i * step, step)], sems.at[i]
            )
        )
        copies[-1].start()
        grad = (cot_ref[here, :].astype(F32) * (gate * (1.0 + pre * (1.0 - gate)))).astype(BF16)
        grad_ref[here, :] = grad
        ht_ref[:, here] = dot_nt(w_ref[...], grad).astype(BF16)
    px_ref[...] = dot(ht_ref[...], a_ref[PLANE_X, :, :end]).T.astype(BF16)
    for copy in copies:
        copy.wait()


def middle(terms, end, *args):
    rows, width = args[2].shape
    wide = pltpu.VMEM((rows, width), BF16)
    return pl.pallas_call(
        functools.partial(middle_kernel, terms, end),
        out_shape=[
            pltpu.HBM((rows, width), BF16), wide, wide, pltpu.VMEM((width, rows), BF16), pltpu.VMEM((end, width), BF16)
        ],
        in_specs=[vmem_spec()] * len(args),
        out_specs=[hbm_spec()] + [vmem_spec()] * 4,
        scratch_shapes=[wide, pltpu.SemaphoreType.DMA((4,))],
        compiler_params=pltpu.CompilerParams(vmem_limit_bytes=LIMIT),
        cost_estimate=COST,
        name="middle",
    )(*[in_vmem(a) for a in args])


def spread_kernel(part, cuts, a_ref, ht_ref, *out_refs):
    for (low, high), out_ref in zip(cuts, out_refs):
        out_ref[...] = dot(ht_ref[...], a_ref[part, :, low:high]).T.astype(out_ref.dtype)


def spread(dense, ht, part, cuts, dtype, name):
    rows, width = dense.shape[1], ht.shape[0]
    return kernel_call(
        functools.partial(spread_kernel, part, cuts),
        name,
        [((high - low, width), dtype) for low, high in cuts],
        [dense, ht],
    )


def spread_two_kernel(low, high, a_ref, ht_ref, px_ref, p_ref):
    for part, out_ref in ((PLANE_X, px_ref), (PLANE, p_ref)):
        out_ref[...] = dot(ht_ref[...], a_ref[part, :, low:high]).T.astype(BF16)


def spread_two(dense, ht, here, name):
    shape = (here[1] - here[0], ht.shape[0])
    return kernel_call(functools.partial(spread_two_kernel, *here), name, [(shape, BF16)] * 2, [dense, ht])


def own_kernel(cuts, a_ref, ht_ref, grad_ref, r_ref, *out_refs):
    for (low, high), out_ref in zip(cuts, out_refs):
        out_ref[...] = dot(ht_ref[...], a_ref[OWN, :, low:high]).T + dot_nt(grad_ref[low:high, :], r_ref[...])


def final_kernel(low, terms, *refs):
    out_ref, chunk_ref, sem = refs[-3:]
    total = refs[0][...]
    for ref in refs[1:terms]:
        total = total + ref[...].astype(F32)
    chunk_ref[...] = total.astype(BF16)
    copy = pltpu.make_async_copy(chunk_ref, out_ref.at[pl.ds(low, chunk_ref.shape[0])], sem)
    copy.start()
    copy.wait()


def final(low, args, rows, result):
    terms = len(args)
    chunk, width = args[0].shape
    return pl.pallas_call(
        functools.partial(final_kernel, low, terms),
        out_shape=pltpu.HBM((rows, width), BF16),
        in_specs=[vmem_spec()] * terms + ([] if result is None else [hbm_spec()]),
        out_specs=hbm_spec(),
        scratch_shapes=[pltpu.VMEM((chunk, width), BF16), pltpu.SemaphoreType.DMA],
        input_output_aliases={} if result is None else {terms: 0},
        compiler_params=pltpu.CompilerParams(vmem_limit_bytes=LIMIT),
        cost_estimate=COST,
        name="final",
    )(*[in_vmem(a) for a in args], *([] if result is None else [in_hbm(result)]))


def relay_kernel(own_ref, other_ref, arrived_ref, out_ref):
    out_ref[...] = (own_ref[...] + other_ref[...].astype(F32) + arrived_ref[...].astype(F32)).astype(BF16)


def relayed(own, other, arrived):
    return kernel_call(relay_kernel, "relay", [(own.shape, BF16)], [own, other, arrived])[0]


def weight_kernel(ax_ref, x_ref, grad_ref, kept_ref, sent_ref):
    core = lax.axis_index("row") & 1
    first = dot_tn(ax_ref[...], grad_ref[...])
    second = dot_tn(x_ref[...], grad_ref[...])
    kept_ref[...] = jnp.where(core == 0, first, second)
    sent_ref[...] = jnp.where(core == 0, second, first)


def scaled_kernel(scale, kept_ref, other_ref, weight_out, root_out, weight_ref, root_ref, sems):
    core = lax.axis_index("row") & 1
    kept, other = kept_ref[...] * scale, other_ref[...] * scale
    weight_ref[...] = jnp.where(core == 0, kept, other)
    root_ref[...] = jnp.where(core == 0, other, kept)
    copies = [
        pltpu.make_async_copy(weight_ref, weight_out, sems.at[0]),
        pltpu.make_async_copy(root_ref, root_out, sems.at[1]),
    ]
    for copy in copies:
        copy.start()
    for copy in copies:
        copy.wait()


def scaled(scale, kept, other):
    shape = kept.shape
    return pl.pallas_call(
        functools.partial(scaled_kernel, scale),
        out_shape=[pltpu.HBM(shape, F32)] * 2,
        in_specs=[vmem_spec()] * 2,
        out_specs=[hbm_spec()] * 2,
        scratch_shapes=[pltpu.VMEM(shape, F32)] * 2 + [pltpu.SemaphoreType.DMA((2,))],
        compiler_params=pltpu.CompilerParams(vmem_limit_bytes=LIMIT),
        cost_estimate=COST,
        name="scaled",
    )(in_vmem(kept), in_vmem(other))


def added(a, b, dtype=BF16):
    return (a.astype(F32) + b.astype(F32)).astype(dtype)


def body(features, weight, root_weight, block_tiles, tile_rows, tile_cols, tile_count, cotangent):
    count = lax.axis_size("row")
    rows, width = features.shape
    split = rows * FORWARD // 16

    side_low = flip_side(cut(features, 0, split), count)
    dense = dense_adjacency(tile_rows, tile_cols, tile_count, block_tiles, rows)
    high = cut(after(features, dense), split, rows)
    side_low, high = lax.optimization_barrier((side_low, high))
    side_high = flip_side(high, count)
    plane_high = past_side(high, count, False)
    plane_low = over_planes(side_low, count, False, True)
    side_x_low = flip_core(side_low, count)
    own_x = flip_core(after(features, side_low), count)
    total = gathered(dense, [(OWN, 0), (OWN_X, 0)], [features, own_x], None, "gather_own")
    total = gathered(dense, [(SIDE, 0), (SIDE_X, 0)], [side_low, side_x_low], total, "gather_side")
    plane_low = after(plane_low, total)
    plane_x_low = flip_core(plane_low, count)
    side_x_high = flip_core(side_high, count)
    plane_x_high = flip_core(plane_high, count)
    total = gathered(dense, [(SIDE, split), (PLANE, split)], [side_high, plane_high], total, "gather_high")
    total = gathered(dense, [(PLANE, 0), (PLANE_X, 0)], [plane_low, plane_x_low], total, "gather_plane")

    split_back = rows * BACKWARD // 16
    back = [(0, split_back), (split_back, rows)]
    layer_out, grad_pre, gathered_x, ht, px_low = middle(
        [(SIDE_X, split, rows), (PLANE_X, split, rows)], split_back,
        dense, total, features, weight, root_weight, cotangent, side_x_high, plane_x_high,
    )

    (p_low,) = spread(dense, ht, PLANE, back[:1], BF16, "spread_plane_low")
    far_low = over_planes(added(p_low, flip_core(px_low, count)), count, True, True)
    px_high, p_high = spread_two(dense, ht, back[1], "spread_plane_high")
    far_high = over_planes(added(p_high, flip_core(px_high, count)), count, True, False)

    square = ((width, width), F32)
    kept, sent = kernel_call(weight_kernel, "weight_products", [square, square], [gathered_x, features, grad_pre])
    kept = kept + flip_core(sent, count)
    mine = kept.astype(BF16)
    kept = added(mine, flip_side(mine, count), F32)

    ht = after(ht, mine)
    sx = [flip_core(share, count) for share in spread(dense, ht, SIDE_X, back, BF16, "spread_side_x")]
    s = spread(dense, ht, SIDE, back, F32, "spread_side")
    ox = [flip_core(share, count) for share in spread(dense, ht, OWN_X, back, BF16, "spread_own_x")]
    own = kernel_call(
        functools.partial(own_kernel, back),
        "spread_own",
        [((high - low, width), F32) for low, high in back],
        [dense, ht, grad_pre, root_weight],
    )
    low = relayed(after(s[0], *own), sx[0], far_low)
    near_low = flip_side(low, count)
    high = relayed(after(s[1], near_low), sx[1], far_high)
    near_high = flip_side(high, count)
    hop, ties = 4, [low, high]
    while hop < count:
        mine = (after(kept, ties.pop(0)) if ties else kept).astype(BF16)
        kept = added(mine, lax.ppermute(mine, "row", [(i, i ^ hop) for i in range(count)]), F32)
        hop *= 2
    grad_features = final(back[0][0], [own[0], ox[0], near_low], rows, None)
    grad_features = final(back[1][0], [own[1], ox[1], near_high], rows, grad_features)
    other = flip_core(kept, count)
    total_weight, total_root = scaled(1.0 / math.sqrt(count * rows), kept, other)

    return layer_out, grad_features, total_weight, total_root


def solution(mesh):
    placed = (
        P(("groups", "row"), None),
        P(),
        P(),
        P(("groups", "row"), None, None),
        P(("groups", "row")),
        P(("groups", "row")),
        P(("groups", "row")),
        P(("groups", "row"), None),
    )
    return jax.shard_map(
        body,
        mesh=mesh,
        in_specs=placed,
        out_specs=(
            P(("groups", "row"), None),
            P(("groups", "row"), None),
            P("groups", None),
            P("groups", None),
        ),
        check_vma=False,
    )
```

```python
import functools
import math

import jax
import jax.numpy as jnp
from jax import lax
from jax.experimental import pallas as pl
from jax.experimental.pallas import tpu as pltpu
from jax.sharding import PartitionSpec as P

REACH = 2
F32, BF16 = jnp.float32, jnp.bfloat16

OWN, OWN_X, SIDE, SIDE_X, PLANE, PLANE_X = range(6)
PARTS = 6
LIMIT = 4 << 20
CUT = 128
SHORT = pl.CostEstimate(flops=0, bytes_accessed=0, transcendentals=0)
LONG = pl.CostEstimate(flops=10**10, bytes_accessed=0, transcendentals=0)
FORWARD = 10


def vmem_spec():
    return pl.BlockSpec(memory_space=pltpu.VMEM)


def after(array, *others):
    return lax.optimization_barrier((array, *others))[0]


def smem_spec():
    return pl.BlockSpec(memory_space=pltpu.SMEM)


def hbm_spec():
    return pl.BlockSpec(memory_space=pltpu.HBM)


def in_vmem(array):
    return pltpu.with_memory_space_constraint(array, pltpu.VMEM)


def in_hbm(array):
    return pltpu.with_memory_space_constraint(array, pltpu.HBM)


def kernel_call(kernel, name, outs, args, cost=SHORT):
    return pl.pallas_call(
        kernel,
        out_shape=[pltpu.VMEM(shape, dtype) for shape, dtype in outs],
        in_specs=[vmem_spec()] * len(args),
        out_specs=[vmem_spec()] * len(outs),
        compiler_params=pltpu.CompilerParams(vmem_limit_bytes=LIMIT),
        cost_estimate=cost,
        name=name,
    )(*[in_vmem(a) for a in args])


def flip_core(array, count):
    return lax.ppermute(array, "row", [(i, i ^ 1) for i in range(count)])


def flip_side(array, count):
    return lax.ppermute(array, "row", [(i, i ^ 2) for i in range(count)])


def over_planes(array, count, back):
    step = [(i, i + 4) for i in range(count) if i % 4 < 2 and i + 4 < count]
    step += [(i, i - 4) for i in range(count) if i % 4 >= 2 and i >= 4]
    if back:
        step = [(b, a) for a, b in step]
        step += [(0, count - 4), (1, count - 3), (count - 2, 2), (count - 1, 3)]
    else:
        step += [(count - 4, count - 2), (count - 3, count - 1), (2, 0), (3, 1)]
    return lax.ppermute(array, "row", step)


def past_side(array, count, back):
    step = [(i, (i ^ 2) + 4) for i in range(count) if i % 4 >= 2 and i + 4 < count]
    step += [(i, (i ^ 2) - 4) for i in range(count) if i % 4 < 2 and i >= 4]
    return lax.ppermute(array, "row", [(b, a) for a, b in step] if back else step)


def dense_kernel(count_ref, rows_hbm, cols_hbm, tiles_ref, a_ref, rows_ref, cols_ref, sem, index_sems):
    block = tiles_ref.shape[1]
    width = a_ref.shape[1]
    blocks = width // block
    fetches = [
        pltpu.make_async_copy(src, dst, index_sems.at[i])
        for i, (src, dst) in enumerate(((rows_hbm, rows_ref), (cols_hbm, cols_ref)))
    ]
    for fetch in fetches:
        fetch.start()
    stripe = lax.axis_index("row")
    core, side = stripe & 1, (stripe >> 1) & 1
    first = (stripe >> 1) * (2 * blocks)

    def clear(i, carry):
        for part in range(PARTS):
            a_ref[part, pl.ds(pl.multiple_of(i * 64, 64), 64), :] = jnp.zeros((64, width), BF16)
        return carry

    def placed(slot):
        away = cols_ref[slot] - first + 2 * blocks
        chip = away // (2 * blocks)
        within = away - chip * (2 * blocks)
        other = within // blocks
        column = within - other * blocks
        near = jnp.where(side == 0, 2, 0)
        part = jnp.where(chip == 1, OWN, jnp.where(chip == near, SIDE, PLANE)) + (other ^ core)
        target = a_ref.at[
            part,
            pl.ds(pl.multiple_of(rows_ref[slot] * block, block), block),
            pl.ds(pl.multiple_of(column * block, block), block),
        ]
        return pltpu.make_async_copy(tiles_ref.at[slot], target, sem)

    def start(slot, carry):
        placed(slot).start()
        return carry

    def finish(slot, carry):
        placed(slot).wait()
        return carry

    lax.fori_loop(0, width // 64, clear, 0)
    for fetch in fetches:
        fetch.wait()
    live = count_ref[0]
    lax.fori_loop(0, live, start, 0)
    lax.fori_loop(0, live, finish, 0)


def dense_adjacency(tile_rows, tile_cols, tile_count, block_tiles, width):
    slots = tile_rows.shape[0]
    return pl.pallas_call(
        dense_kernel,
        out_shape=pltpu.VMEM((PARTS, width, width), BF16),
        in_specs=[smem_spec()] + [hbm_spec()] * 3,
        out_specs=vmem_spec(),
        scratch_shapes=[
            pltpu.SMEM((slots,), jnp.int32),
            pltpu.SMEM((slots,), jnp.int32),
            pltpu.SemaphoreType.DMA,
            pltpu.SemaphoreType.DMA((2,)),
        ],
        compiler_params=pltpu.CompilerParams(vmem_limit_bytes=LIMIT),
        cost_estimate=SHORT,
        name="dense_adjacency",
    )(tile_count, *[in_hbm(a) for a in (tile_rows, tile_cols, block_tiles)])


def dot(a, b):
    return jnp.dot(a, b, preferred_element_type=F32)


def dot_nt(a, b):
    return lax.dot_general(a, b, (((1,), (1,)), ((), ())), preferred_element_type=F32)


def dot_tn(a, b):
    return lax.dot_general(a, b, (((0,), (0,)), ((), ())), preferred_element_type=F32)


def gather_kernel(terms, started, *refs):
    a_ref, out_ref = refs[0], refs[-1]
    sources = refs[1:-1]
    total = sources[-1][...] if started else None
    for (part, low), source in zip(terms, sources):
        product = dot(a_ref[part, :, low : low + source.shape[0]], source[...])
        total = product if total is None else total + product
    out_ref[...] = total


def gathered(dense, terms, sources, total, name, cost=SHORT):
    rows, width = dense.shape[1], sources[0].shape[1]
    args = [dense, *sources] + ([] if total is None else [total])
    return kernel_call(
        functools.partial(gather_kernel, terms, total is not None), name, [((rows, width), F32)], args, cost
    )[0]


def cut_kernel(at, src_ref, out_ref, sems):
    copies = []
    rows = out_ref.shape[0]
    for i, low in enumerate(range(0, rows, CUT)):
        size = min(CUT, rows - low)
        copies.append(
            pltpu.make_async_copy(src_ref.at[pl.ds(at + low, size)], out_ref.at[pl.ds(low, size)], sems.at[i])
        )
    for copy in copies:
        copy.start()
    for copy in copies:
        copy.wait()


def cut(array, at, end):
    return pl.pallas_call(
        functools.partial(cut_kernel, at),
        out_shape=pltpu.VMEM((end - at, array.shape[1]), array.dtype),
        in_specs=[hbm_spec()],
        out_specs=vmem_spec(),
        scratch_shapes=[pltpu.SemaphoreType.DMA((pl.cdiv(end - at, CUT),))],
        compiler_params=pltpu.CompilerParams(vmem_limit_bytes=LIMIT),
        cost_estimate=SHORT,
        name="cut",
    )(in_hbm(array))


def middle_kernel(terms, a_ref, total_ref, x_ref, w_ref, r_ref, cot_ref, *refs):
    last_refs, refs = refs[: len(terms)], refs[len(terms) :]
    out_hbm, grad_ref, ax_ref, ht_ref, px_ref, out_ref, sems = refs
    rows = x_ref.shape[0]
    step = rows // sems.shape[0]
    copies = []
    for i in range(sems.shape[0]):
        here = slice(i * step, (i + 1) * step)
        ax = total_ref[here, :]
        for (part, low, high), last_ref in zip(terms, last_refs):
            ax = ax + dot(a_ref[part, here, low:high], last_ref[...])
        ax = ax.astype(BF16)
        ax_ref[here, :] = ax
        pre = dot(ax, w_ref[...]) + dot(x_ref[here, :], r_ref[...])
        gate = jax.nn.sigmoid(pre)
        out_ref[here, :] = (pre * gate).astype(BF16)
        copies.append(
            pltpu.make_async_copy(
                out_ref.at[pl.ds(i * step, step)], out_hbm.at[pl.ds(i * step, step)], sems.at[i]
            )
        )
        copies[-1].start()
        grad = (cot_ref[here, :].astype(F32) * (gate * (1.0 + pre * (1.0 - gate)))).astype(BF16)
        grad_ref[here, :] = grad
        ht_ref[:, here] = dot_nt(w_ref[...], grad).astype(BF16)
    px_ref[...] = dot(ht_ref[...], a_ref[PLANE_X, :, :]).T.astype(BF16)
    for copy in copies:
        copy.wait()


def middle(terms, *args):
    rows, width = args[2].shape
    wide = pltpu.VMEM((rows, width), BF16)
    return pl.pallas_call(
        functools.partial(middle_kernel, terms),
        out_shape=[
            pltpu.HBM((rows, width), BF16), wide, wide, pltpu.VMEM((width, rows), BF16), wide
        ],
        in_specs=[vmem_spec()] * len(args),
        out_specs=[hbm_spec()] + [vmem_spec()] * 4,
        scratch_shapes=[wide, pltpu.SemaphoreType.DMA((4,))],
        compiler_params=pltpu.CompilerParams(vmem_limit_bytes=LIMIT),
        cost_estimate=SHORT,
        name="middle",
    )(*[in_vmem(a) for a in args])


def spread_kernel(part, a_ref, ht_ref, out_ref):
    half = out_ref.shape[0] // 2
    for here in (slice(0, half), slice(half, None)):
        out_ref[here, :] = dot(ht_ref[...], a_ref[part, :, here]).T.astype(out_ref.dtype)


def spread(dense, ht, part, dtype, name):
    shape = (dense.shape[1], ht.shape[0])
    return kernel_call(functools.partial(spread_kernel, part), name, [(shape, dtype)], [dense, ht])[0]


def own_kernel(a_ref, ht_ref, grad_ref, r_ref, out_ref):
    half = out_ref.shape[0] // 2
    for here in (slice(0, half), slice(half, None)):
        out_ref[here, :] = dot(ht_ref[...], a_ref[OWN, :, here]).T + dot_nt(grad_ref[here, :], r_ref[...])


def final_kernel(own_ref, other_ref, arrived_ref, out_ref):
    out_ref[...] = (own_ref[...] + other_ref[...].astype(F32) + arrived_ref[...].astype(F32)).astype(BF16)


def scaled_kernel(
    scale, out_ref, kept_ref, other_ref, out_hbm, weight_hbm, root_hbm, weight_ref, root_ref, sems
):
    copies = [pltpu.make_async_copy(out_ref, out_hbm, sems.at[0])]
    copies[0].start()
    core = lax.axis_index("row") & 1
    kept, other = kept_ref[...] * scale, other_ref[...] * scale
    weight_ref[...] = jnp.where(core == 0, kept, other)
    root_ref[...] = jnp.where(core == 0, other, kept)
    copies.append(pltpu.make_async_copy(weight_ref, weight_hbm, sems.at[1]))
    copies.append(pltpu.make_async_copy(root_ref, root_hbm, sems.at[2]))
    for copy in copies[1:]:
        copy.start()
    for copy in copies:
        copy.wait()


def scaled(scale, result, kept, other):
    shape = kept.shape
    return pl.pallas_call(
        functools.partial(scaled_kernel, scale),
        out_shape=[pltpu.HBM(result.shape, BF16), pltpu.HBM(shape, F32), pltpu.HBM(shape, F32)],
        in_specs=[vmem_spec()] * 3,
        out_specs=[hbm_spec()] * 3,
        scratch_shapes=[pltpu.VMEM(shape, F32)] * 2 + [pltpu.SemaphoreType.DMA((3,))],
        compiler_params=pltpu.CompilerParams(vmem_limit_bytes=LIMIT),
        cost_estimate=SHORT,
        name="scaled",
    )(in_vmem(result), in_vmem(kept), in_vmem(other))


def relay_kernel(own_ref, arrived_ref, out_ref):
    out_ref[...] = own_ref[...] + arrived_ref[...].astype(F32)


def relayed(own, arrived):
    return kernel_call(relay_kernel, "relay", [(own.shape, F32)], [own, arrived], LONG)[0]


def weight_kernel(ax_ref, x_ref, grad_ref, kept_ref, sent_ref):
    core = lax.axis_index("row") & 1
    first = dot_tn(ax_ref[...], grad_ref[...])
    second = dot_tn(x_ref[...], grad_ref[...])
    kept_ref[...] = jnp.where(core == 0, first, second)
    sent_ref[...] = jnp.where(core == 0, second, first)


def exchanged(kept, hop, count):
    mine = kept.astype(BF16)
    return added(mine, lax.ppermute(mine, "row", [(i, i ^ hop) for i in range(count)]), F32)


def added(a, b, dtype=BF16):
    return (a.astype(F32) + b.astype(F32)).astype(dtype)


def body(features, weight, root_weight, block_tiles, tile_rows, tile_cols, tile_count, cotangent):
    count = lax.axis_size("row")
    rows, width = features.shape
    split = rows * FORWARD // 16

    side_low = flip_side(cut(features, 0, split), count)
    dense = dense_adjacency(tile_rows, tile_cols, tile_count, block_tiles, rows)
    high = cut(after(features, dense), split, rows)
    side_low, high = lax.optimization_barrier((side_low, high))
    side_high = flip_side(high, count)
    plane_high = past_side(high, count, False)
    plane_low = over_planes(side_low, count, False)
    side_x_low = flip_core(side_low, count)
    own_x = flip_core(after(features, side_low), count)
    total = gathered(dense, [(OWN, 0), (OWN_X, 0)], [features, own_x], None, "gather_own")
    total = gathered(dense, [(SIDE, 0), (SIDE_X, 0)], [side_low, side_x_low], total, "gather_side")
    plane_low = after(plane_low, total)
    plane_x_low = flip_core(plane_low, count)
    side_x_high = flip_core(side_high, count)
    plane_x_high = flip_core(plane_high, count)
    total = gathered(dense, [(SIDE, split), (PLANE, split)], [side_high, plane_high], total, "gather_high")
    total = gathered(dense, [(PLANE, 0), (PLANE_X, 0)], [plane_low, plane_x_low], total, "gather_plane")

    layer_out, grad_pre, gathered_x, ht, px = middle(
        [(SIDE_X, split, rows), (PLANE_X, split, rows)],
        dense, total, features, weight, root_weight, cotangent, side_x_high, plane_x_high,
    )

    share = added(spread(dense, ht, PLANE, BF16, "spread_plane"), flip_core(px, count))
    far = over_planes(share, count, True)

    square = ((width, width), F32)
    kept, sent = kernel_call(weight_kernel, "weight_products", [square, square], [gathered_x, features, grad_pre])
    kept = kept + flip_core(sent, count)
    kept = exchanged(kept, 2, count)

    ht = after(ht, share)
    sx = flip_core(spread(dense, ht, SIDE_X, BF16, "spread_side_x"), count)
    s = spread(dense, ht, SIDE, F32, "spread_side")
    ox = spread(dense, ht, OWN_X, BF16, "spread_own_x")
    own = kernel_call(own_kernel, "spread_own", [((rows, width), F32)], [dense, ht, grad_pre, root_weight])[0]
    through = added(relayed(after(s, own, ox), far), sx)
    near = flip_side(through, count)
    kept = after(kept, through)
    hop = 4
    while hop < count:
        kept = exchanged(kept, hop, count)
        hop *= 2
    result = kernel_call(final_kernel, "final", [((rows, width), BF16)], [own, flip_core(ox, count), near], LONG)[0]
    grad_features, total_weight, total_root = scaled(
        1.0 / math.sqrt(count * rows), result, kept, flip_core(kept, count)
    )
    return layer_out, grad_features, total_weight, total_root


def solution(mesh):
    placed = (
        P(("groups", "row"), None),
        P(),
        P(),
        P(("groups", "row"), None, None),
        P(("groups", "row")),
        P(("groups", "row")),
        P(("groups", "row")),
        P(("groups", "row"), None),
    )
    return jax.shard_map(
        body,
        mesh=mesh,
        in_specs=placed,
        out_specs=(
            P(("groups", "row"), None),
            P(("groups", "row"), None),
            P("groups", None),
            P("groups", None),
        ),
        check_vma=False,
    )
```

```python
import functools
import math

import jax
import jax.numpy as jnp
from jax import lax
from jax.experimental import pallas as pl
from jax.experimental.pallas import tpu as pltpu
from jax.sharding import PartitionSpec as P

REACH = 2
F32, BF16 = jnp.float32, jnp.bfloat16

OWN, OWN_X, SIDE, SIDE_X, PLANE, PLANE_X = range(6)
PARTS = 6
LIMIT = 4 << 20
CUT = 64
SHORT = pl.CostEstimate(flops=0, bytes_accessed=0, transcendentals=0)
RELAY = pl.CostEstimate(flops=10**10, bytes_accessed=0, transcendentals=0)
LONG = pl.CostEstimate(flops=10**10, bytes_accessed=0, transcendentals=0)
FORWARD = 11
BACKWARD = 12


def vmem_spec():
    return pl.BlockSpec(memory_space=pltpu.VMEM)


def after(array, *others):
    return lax.optimization_barrier((array, *others))[0]


def smem_spec():
    return pl.BlockSpec(memory_space=pltpu.SMEM)


def hbm_spec():
    return pl.BlockSpec(memory_space=pltpu.HBM)


def in_vmem(array):
    return pltpu.with_memory_space_constraint(array, pltpu.VMEM)


def in_hbm(array):
    return pltpu.with_memory_space_constraint(array, pltpu.HBM)


def kernel_call(kernel, name, outs, args, cost=SHORT):
    return pl.pallas_call(
        kernel,
        out_shape=[pltpu.VMEM(shape, dtype) for shape, dtype in outs],
        in_specs=[vmem_spec()] * len(args),
        out_specs=[vmem_spec()] * len(outs),
        compiler_params=pltpu.CompilerParams(vmem_limit_bytes=LIMIT),
        cost_estimate=cost,
        name=name,
    )(*[in_vmem(a) for a in args])


def flip_core(array, count):
    return lax.ppermute(array, "row", [(i, i ^ 1) for i in range(count)])


def flip_side(array, count):
    return lax.ppermute(array, "row", [(i, i ^ 2) for i in range(count)])


def over_planes(array, count, back, ends):
    step = [(i, i + 4) for i in range(count) if i % 4 < 2 and i + 4 < count]
    step += [(i, i - 4) for i in range(count) if i % 4 >= 2 and i >= 4]
    if ends == "around":
        step += [(count - 4, 0), (count - 3, 1), (2, count - 2), (3, count - 1)]
    elif ends == "side":
        step += [(count - 4, count - 2), (count - 3, count - 1), (2, 0), (3, 1)]
    return lax.ppermute(array, "row", [(b, a) for a, b in step] if back else step)


def dense_kernel(count_ref, rows_hbm, cols_hbm, tiles_ref, a_ref, rows_ref, cols_ref, sem, index_sems):
    block = tiles_ref.shape[1]
    width = a_ref.shape[1]
    blocks = width // block
    fetches = [
        pltpu.make_async_copy(src, dst, index_sems.at[i])
        for i, (src, dst) in enumerate(((rows_hbm, rows_ref), (cols_hbm, cols_ref)))
    ]
    for fetch in fetches:
        fetch.start()
    stripe = lax.axis_index("row")
    core, side = stripe & 1, (stripe >> 1) & 1
    first = (stripe >> 1) * (2 * blocks)

    def clear(i, carry):
        for part in range(PARTS):
            a_ref[part, pl.ds(pl.multiple_of(i * 64, 64), 64), :] = jnp.zeros((64, width), BF16)
        return carry

    def placed(slot):
        away = cols_ref[slot] - first + 2 * blocks
        chip = away // (2 * blocks)
        within = away - chip * (2 * blocks)
        other = within // blocks
        column = within - other * blocks
        near = jnp.where(side == 0, 2, 0)
        part = jnp.where(chip == 1, OWN, jnp.where(chip == near, SIDE, PLANE)) + (other ^ core)
        target = a_ref.at[
            part,
            pl.ds(pl.multiple_of(rows_ref[slot] * block, block), block),
            pl.ds(pl.multiple_of(column * block, block), block),
        ]
        return pltpu.make_async_copy(tiles_ref.at[slot], target, sem)

    def start(slot, carry):
        placed(slot).start()
        return carry

    def finish(slot, carry):
        placed(slot).wait()
        return carry

    lax.fori_loop(0, width // 64, clear, 0)
    for fetch in fetches:
        fetch.wait()
    live = count_ref[0]
    lax.fori_loop(0, live, start, 0)
    lax.fori_loop(0, live, finish, 0)


def dense_adjacency(tile_rows, tile_cols, tile_count, block_tiles, width):
    slots = tile_rows.shape[0]
    return pl.pallas_call(
        dense_kernel,
        out_shape=pltpu.VMEM((PARTS, width, width), BF16),
        in_specs=[smem_spec()] + [hbm_spec()] * 3,
        out_specs=vmem_spec(),
        scratch_shapes=[
            pltpu.SMEM((slots,), jnp.int32),
            pltpu.SMEM((slots,), jnp.int32),
            pltpu.SemaphoreType.DMA,
            pltpu.SemaphoreType.DMA((2,)),
        ],
        compiler_params=pltpu.CompilerParams(vmem_limit_bytes=LIMIT),
        cost_estimate=SHORT,
        name="dense_adjacency",
    )(tile_count, *[in_hbm(a) for a in (tile_rows, tile_cols, block_tiles)])


def dot(a, b):
    return jnp.dot(a, b, preferred_element_type=F32)


def dot_nt(a, b):
    return lax.dot_general(a, b, (((1,), (1,)), ((), ())), preferred_element_type=F32)


def dot_tn(a, b):
    return lax.dot_general(a, b, (((0,), (0,)), ((), ())), preferred_element_type=F32)


def gather_kernel(terms, started, *refs):
    a_ref, out_ref = refs[0], refs[-1]
    sources = refs[1:-1]
    total = sources[-1][...] if started else None
    for (part, low, high, at), source in zip(terms, sources):
        product = dot(a_ref[part, :, low:high], source[at : at + high - low, :])
        total = product if total is None else total + product
    out_ref[...] = total


def gathered(dense, terms, sources, total, name, cost=SHORT):
    rows, width = dense.shape[1], sources[0].shape[1]
    args = [dense, *sources] + ([] if total is None else [total])
    return kernel_call(
        functools.partial(gather_kernel, terms, total is not None), name, [((rows, width), F32)], args, cost
    )[0]


def cut_kernel(split, src_ref, low_ref, high_ref, sems):
    copies = []
    for i, low in enumerate(range(0, src_ref.shape[0], CUT)):
        target = low_ref.at[pl.ds(low, CUT)] if low < split else high_ref.at[pl.ds(low - split, CUT)]
        copies.append(pltpu.make_async_copy(src_ref.at[pl.ds(low, CUT)], target, sems.at[i]))
    for copy in copies:
        copy.start()
    for copy in copies:
        copy.wait()


def cut(array, split):
    rows, width = array.shape
    return pl.pallas_call(
        functools.partial(cut_kernel, split),
        out_shape=[pltpu.VMEM((split, width), array.dtype), pltpu.VMEM((rows - split, width), array.dtype)],
        in_specs=[hbm_spec()],
        out_specs=[vmem_spec()] * 2,
        scratch_shapes=[pltpu.SemaphoreType.DMA((rows // CUT,))],
        compiler_params=pltpu.CompilerParams(vmem_limit_bytes=LIMIT),
        cost_estimate=SHORT,
        name="cut",
    )(in_hbm(array))


def join_kernel(a_ref, b_ref, out_ref):
    rows = a_ref.shape[0]
    out_ref[:rows, :] = a_ref[...]
    out_ref[rows:, :] = b_ref[...]


def middle_kernel(terms, end, a_ref, total_ref, x_ref, w_ref, r_ref, cot_ref, *refs):
    last_ref, *refs = refs
    out_hbm, grad_ref, ax_ref, ht_ref, low_ref, high_ref, out_ref, sems = refs
    rows = x_ref.shape[0]
    step = rows // sems.shape[0]
    copies = []
    for i in range(sems.shape[0]):
        here = slice(i * step, (i + 1) * step)
        ax = total_ref[here, :]
        at = 0
        for part, low, high in terms:
            ax = ax + dot(a_ref[part, here, low:high], last_ref[at : at + high - low, :])
            at += high - low
        ax = ax.astype(BF16)
        ax_ref[here, :] = ax
        pre = dot(ax, w_ref[...]) + dot(x_ref[here, :], r_ref[...])
        gate = jax.nn.sigmoid(pre)
        out_ref[here, :] = (pre * gate).astype(BF16)
        copies.append(
            pltpu.make_async_copy(
                out_ref.at[pl.ds(i * step, step)], out_hbm.at[pl.ds(i * step, step)], sems.at[i]
            )
        )
        copies[-1].start()
        grad = (cot_ref[here, :].astype(F32) * (gate * (1.0 + pre * (1.0 - gate)))).astype(BF16)
        grad_ref[here, :] = grad
        ht_ref[:, here] = dot_nt(w_ref[...], grad).astype(BF16)
    low_ref[...] = dot(ht_ref[...], a_ref[PLANE_X, :, :end]).T.astype(BF16)
    high_ref[...] = dot(ht_ref[...], a_ref[PLANE_X, :, end:]).T.astype(BF16)
    for copy in copies:
        copy.wait()


def middle(terms, end, *args):
    rows, width = args[2].shape
    wide = pltpu.VMEM((rows, width), BF16)
    return pl.pallas_call(
        functools.partial(middle_kernel, terms, end),
        out_shape=[
            pltpu.HBM((rows, width), BF16), wide, wide, pltpu.VMEM((width, rows), BF16),
            pltpu.VMEM((end, width), BF16), pltpu.VMEM((rows - end, width), BF16),
        ],
        in_specs=[vmem_spec()] * len(args),
        out_specs=[hbm_spec()] + [vmem_spec()] * 5,
        scratch_shapes=[wide, pltpu.SemaphoreType.DMA((4,))],
        compiler_params=pltpu.CompilerParams(vmem_limit_bytes=LIMIT),
        cost_estimate=SHORT,
        name="middle",
    )(*[in_vmem(a) for a in args])


def spread_kernel(part, cuts, a_ref, ht_ref, *out_refs):
    for (low, high), out_ref in zip(cuts, out_refs):
        out_ref[...] = dot(ht_ref[...], a_ref[part, :, low:high]).T.astype(out_ref.dtype)


def spread(dense, ht, part, cuts, dtype, name):
    outs = [((high - low, ht.shape[0]), dtype) for low, high in cuts]
    return kernel_call(functools.partial(spread_kernel, part, cuts), name, outs, [dense, ht])


def pack_kernel(share_ref, other_ref, kept_ref, arrived_ref, out_ref):
    rows = share_ref.shape[0]
    out_ref[:rows, :] = (share_ref[...].astype(F32) + other_ref[...].astype(F32)).astype(BF16)
    out_ref[rows:, :] = (kept_ref[...] + arrived_ref[...]).astype(BF16)


def unpack_kernel(packed_ref, arrived_ref, share_ref, sum_ref):
    rows = share_ref.shape[0]
    share_ref[...] = arrived_ref[:rows, :]
    sum_ref[...] = (packed_ref[rows:, :].astype(F32) + arrived_ref[rows:, :].astype(F32)).astype(BF16)


def own_kernel(a_ref, ht_ref, grad_ref, r_ref, out_ref):
    half = out_ref.shape[0] // 2
    for here in (slice(0, half), slice(half, None)):
        out_ref[here, :] = dot(ht_ref[...], a_ref[OWN, :, here]).T + dot_nt(grad_ref[here, :], r_ref[...])


def final_kernel(split, own_ref, other_ref, low_ref, high_ref, direct_ref, out_ref):
    for rows, refs in ((slice(0, split), (low_ref,)), (slice(split, None), (high_ref, direct_ref))):
        total = own_ref[rows, :] + other_ref[rows, :].astype(F32)
        for ref in refs:
            total = total + ref[...].astype(F32)
        out_ref[rows, :] = total.astype(BF16)


def scaled_kernel(
    scale, out_ref, kept_ref, other_ref, out_hbm, weight_hbm, root_hbm, weight_ref, root_ref, sems
):
    copies = [pltpu.make_async_copy(out_ref, out_hbm, sems.at[0])]
    copies[0].start()
    core = lax.axis_index("row") & 1
    kept, other = kept_ref[...] * scale, other_ref[...] * scale
    weight_ref[...] = jnp.where(core == 0, kept, other)
    root_ref[...] = jnp.where(core == 0, other, kept)
    copies.append(pltpu.make_async_copy(weight_ref, weight_hbm, sems.at[1]))
    copies.append(pltpu.make_async_copy(root_ref, root_hbm, sems.at[2]))
    for copy in copies[1:]:
        copy.start()
    for copy in copies:
        copy.wait()


def scaled(scale, result, kept, other):
    shape = kept.shape
    return pl.pallas_call(
        functools.partial(scaled_kernel, scale),
        out_shape=[pltpu.HBM(result.shape, BF16), pltpu.HBM(shape, F32), pltpu.HBM(shape, F32)],
        in_specs=[vmem_spec()] * 3,
        out_specs=[hbm_spec()] * 3,
        scratch_shapes=[pltpu.VMEM(shape, F32)] * 2 + [pltpu.SemaphoreType.DMA((3,))],
        compiler_params=pltpu.CompilerParams(vmem_limit_bytes=LIMIT),
        cost_estimate=SHORT,
        name="scaled",
    )(in_vmem(result), in_vmem(kept), in_vmem(other))


def relay_kernel(own_ref, arrived_ref, out_ref):
    out_ref[...] = own_ref[...] + arrived_ref[...].astype(F32)


def relayed(own, arrived):
    return kernel_call(relay_kernel, "relay", [(own.shape, F32)], [own, arrived], RELAY)[0]


def weight_kernel(ax_ref, x_ref, grad_ref, kept_ref, sent_ref):
    core = lax.axis_index("row") & 1
    first = dot_tn(ax_ref[...], grad_ref[...])
    second = dot_tn(x_ref[...], grad_ref[...])
    kept_ref[...] = jnp.where(core == 0, first, second)
    sent_ref[...] = jnp.where(core == 0, second, first)


def exchanged(kept, hop, count):
    mine = kept.astype(BF16)
    return added(mine, lax.ppermute(mine, "row", [(i, i ^ hop) for i in range(count)]), F32)


def added(a, b, dtype=BF16):
    return (a.astype(F32) + b.astype(F32)).astype(dtype)


def body(features, weight, root_weight, block_tiles, tile_rows, tile_cols, tile_count, cotangent):
    count = lax.axis_size("row")
    rows, width = features.shape
    split = rows * FORWARD // 16

    low, high = cut(features, split)
    side_low = flip_side(low, count)
    passing = over_planes(high, count, True, "around")
    dense = dense_adjacency(tile_rows, tile_cols, tile_count, block_tiles, rows)
    joined = kernel_call(join_kernel, "join", [((2 * (rows - split), width), BF16)], [high, after(passing, dense)])[0]
    highs = flip_side(joined, count)
    side_low = after(side_low, joined)
    plane_low = over_planes(side_low, count, False, "around")
    side_x_low = flip_core(side_low, count)
    own_x = flip_core(after(features, side_low), count)
    whole, first, rest = (0, rows, 0), (0, split, 0), (split, rows, 0)
    total = gathered(dense, [(OWN, *whole), (OWN_X, *whole)], [features, own_x], None, "gather_own")
    total = gathered(dense, [(SIDE, *first), (SIDE_X, *first)], [side_low, side_x_low], total, "gather_side")
    plane_low = after(plane_low, total)
    plane_x_low = flip_core(plane_low, count)
    highs_x = flip_core(highs, count)
    total = gathered(dense, [(SIDE, *rest), (PLANE, split, rows, rows - split)], [highs, highs], total, "gather_high")
    total = gathered(dense, [(PLANE, *first), (PLANE_X, *first)], [plane_low, plane_x_low], total, "gather_plane")

    split_back = rows * BACKWARD // 16
    back = [(0, split_back), (split_back, rows)]
    layer_out, grad_pre, gathered_x, ht, px_low, px_high = middle(
        [(SIDE_X, split, rows), (PLANE_X, split, rows)], split_back,
        dense, total, features, weight, root_weight, cotangent, highs_x,
    )

    (p_low,) = spread(dense, ht, PLANE, back[:1], BF16, "spread_plane_low")
    p_low = added(p_low, flip_core(px_low, count))
    far = over_planes(p_low, count, True, "around")
    (p_high,) = spread(dense, after(ht, p_low), PLANE, back[1:], BF16, "spread_plane_high")

    square = ((width, width), F32)
    kept, sent = kernel_call(weight_kernel, "weight_products", [square, square], [gathered_x, features, grad_pre])
    high, wide = rows - split_back, (width, width)
    packed = kernel_call(
        pack_kernel, "pack", [((high + width, width), BF16)], [p_high, flip_core(px_high, count), kept, flip_core(sent, count)]
    )[0]
    passing, mine = kernel_call(
        unpack_kernel, "unpack", [((high, width), BF16), (wide, BF16)], [packed, flip_side(packed, count)]
    )

    ht = after(ht, packed)
    sx_low, sx_high = [flip_core(part, count) for part in spread(dense, ht, SIDE_X, back, BF16, "spread_side_x")]
    s_low, s_high = spread(dense, ht, SIDE, back, F32, "spread_side")
    s_high = added(s_high, sx_high)
    near_high = flip_side(s_high, count)
    ht = after(ht, s_high)
    (ox,) = spread(dense, ht, OWN_X, [(0, rows)], BF16, "spread_own_x")
    own = kernel_call(own_kernel, "spread_own", [((rows, width), F32)], [dense, ht, grad_pre, root_weight])[0]
    through = added(relayed(after(s_low, own, ox, near_high), far), sx_low)
    near_low = flip_side(through, count)
    direct = over_planes(passing, count, False, None)
    theirs = lax.ppermute(after(mine, own), "row", [(i, i ^ 4) for i in range(count)])
    kept = added(mine, after(theirs, through), F32)
    hop = 8
    while hop < count:
        kept = exchanged(kept, hop, count)
        hop *= 2
    result = kernel_call(
        functools.partial(final_kernel, split_back), "final", [((rows, width), BF16)],
        [own, flip_core(ox, count), near_low, near_high, direct], LONG,
    )[0]
    grad_features, total_weight, total_root = scaled(
        1.0 / math.sqrt(count * rows), result, kept, flip_core(kept, count)
    )
    return layer_out, grad_features, total_weight, total_root


def solution(mesh):
    placed = (
        P(("groups", "row"), None),
        P(),
        P(),
        P(("groups", "row"), None, None),
        P(("groups", "row")),
        P(("groups", "row")),
        P(("groups", "row")),
        P(("groups", "row"), None),
    )
    return jax.shard_map(
        body,
        mesh=mesh,
        in_specs=placed,
        out_specs=(
            P(("groups", "row"), None),
            P(("groups", "row"), None),
            P("groups", None),
            P("groups", None),
        ),
        check_vma=False,
    )
```

```python
import functools
import math

import jax
import jax.numpy as jnp
from jax import lax
from jax.experimental import pallas as pl
from jax.experimental.pallas import tpu as pltpu
from jax.sharding import PartitionSpec as P

REACH = 2
F32, BF16 = jnp.float32, jnp.bfloat16

OWN, OWN_X, SIDE, SIDE_X, PLANE, PLANE_X = range(6)
PARTS = 6
LIMIT = 4 << 20
CUT = 64
SHORT = pl.CostEstimate(flops=0, bytes_accessed=0, transcendentals=0)
RELAY = pl.CostEstimate(flops=10**10, bytes_accessed=0, transcendentals=0)
BRIEF = pl.CostEstimate(flops=5 * 10**8, bytes_accessed=0, transcendentals=0)
LONG = pl.CostEstimate(flops=10**10, bytes_accessed=0, transcendentals=0)
FORWARD = 10
BACKWARD = 12


def vmem_spec():
    return pl.BlockSpec(memory_space=pltpu.VMEM)


def after(array, *others):
    return lax.optimization_barrier((array, *others))[0]


def smem_spec():
    return pl.BlockSpec(memory_space=pltpu.SMEM)


def hbm_spec():
    return pl.BlockSpec(memory_space=pltpu.HBM)


def in_vmem(array):
    return pltpu.with_memory_space_constraint(array, pltpu.VMEM)


def in_hbm(array):
    return pltpu.with_memory_space_constraint(array, pltpu.HBM)


def kernel_call(kernel, name, outs, args, cost=SHORT):
    return pl.pallas_call(
        kernel,
        out_shape=[pltpu.VMEM(shape, dtype) for shape, dtype in outs],
        in_specs=[vmem_spec()] * len(args),
        out_specs=[vmem_spec()] * len(outs),
        compiler_params=pltpu.CompilerParams(vmem_limit_bytes=LIMIT),
        cost_estimate=cost,
        name=name,
    )(*[in_vmem(a) for a in args])


def flip_core(array, count):
    return lax.ppermute(array, "row", [(i, i ^ 1) for i in range(count)])


def flip_side(array, count):
    return lax.ppermute(array, "row", [(i, i ^ 2) for i in range(count)])


def over_planes(array, count, back, ends):
    step = [(i, i + 4) for i in range(count) if i % 4 < 2 and i + 4 < count]
    step += [(i, i - 4) for i in range(count) if i % 4 >= 2 and i >= 4]
    if ends == "around":
        step += [(count - 4, 0), (count - 3, 1), (2, count - 2), (3, count - 1)]
    elif ends == "side":
        step += [(count - 4, count - 2), (count - 3, count - 1), (2, 0), (3, 1)]
    return lax.ppermute(array, "row", [(b, a) for a, b in step] if back else step)


def dense_kernel(count_ref, rows_hbm, cols_hbm, tiles_ref, a_ref, rows_ref, cols_ref, sem, index_sems):
    block = tiles_ref.shape[1]
    width = a_ref.shape[1]
    blocks = width // block
    fetches = [
        pltpu.make_async_copy(src, dst, index_sems.at[i])
        for i, (src, dst) in enumerate(((rows_hbm, rows_ref), (cols_hbm, cols_ref)))
    ]
    for fetch in fetches:
        fetch.start()
    stripe = lax.axis_index("row")
    core, side = stripe & 1, (stripe >> 1) & 1
    first = (stripe >> 1) * (2 * blocks)

    def clear(i, carry):
        for part in range(PARTS):
            a_ref[part, pl.ds(pl.multiple_of(i * 64, 64), 64), :] = jnp.zeros((64, width), BF16)
        return carry

    def placed(slot):
        away = cols_ref[slot] - first + 2 * blocks
        chip = away // (2 * blocks)
        within = away - chip * (2 * blocks)
        other = within // blocks
        column = within - other * blocks
        near = jnp.where(side == 0, 2, 0)
        part = jnp.where(chip == 1, OWN, jnp.where(chip == near, SIDE, PLANE)) + (other ^ core)
        target = a_ref.at[
            part,
            pl.ds(pl.multiple_of(rows_ref[slot] * block, block), block),
            pl.ds(pl.multiple_of(column * block, block), block),
        ]
        return pltpu.make_async_copy(tiles_ref.at[slot], target, sem)

    def start(slot, carry):
        placed(slot).start()
        return carry

    def finish(slot, carry):
        placed(slot).wait()
        return carry

    lax.fori_loop(0, width // 64, clear, 0)
    for fetch in fetches:
        fetch.wait()
    live = count_ref[0]
    lax.fori_loop(0, live, start, 0)
    lax.fori_loop(0, live, finish, 0)


def dense_adjacency(tile_rows, tile_cols, tile_count, block_tiles, width):
    slots = tile_rows.shape[0]
    return pl.pallas_call(
        dense_kernel,
        out_shape=pltpu.VMEM((PARTS, width, width), BF16),
        in_specs=[smem_spec()] + [hbm_spec()] * 3,
        out_specs=vmem_spec(),
        scratch_shapes=[
            pltpu.SMEM((slots,), jnp.int32),
            pltpu.SMEM((slots,), jnp.int32),
            pltpu.SemaphoreType.DMA,
            pltpu.SemaphoreType.DMA((2,)),
        ],
        compiler_params=pltpu.CompilerParams(vmem_limit_bytes=LIMIT),
        cost_estimate=SHORT,
        name="dense_adjacency",
    )(tile_count, *[in_hbm(a) for a in (tile_rows, tile_cols, block_tiles)])


def dot(a, b):
    return jnp.dot(a, b, preferred_element_type=F32)


def dot_nt(a, b):
    return lax.dot_general(a, b, (((1,), (1,)), ((), ())), preferred_element_type=F32)


def dot_tn(a, b):
    return lax.dot_general(a, b, (((0,), (0,)), ((), ())), preferred_element_type=F32)


def gather_kernel(terms, started, *refs):
    a_ref, out_ref = refs[0], refs[-1]
    sources = refs[1:-1]
    total = sources[-1][...] if started else None
    for (part, low, high, at), source in zip(terms, sources):
        product = dot(a_ref[part, :, low:high], source[at : at + high - low, :])
        total = product if total is None else total + product
    out_ref[...] = total


def gathered(dense, terms, sources, total, name, cost=SHORT):
    rows, width = dense.shape[1], sources[0].shape[1]
    args = [dense, *sources] + ([] if total is None else [total])
    return kernel_call(
        functools.partial(gather_kernel, terms, total is not None), name, [((rows, width), F32)], args, cost
    )[0]


def cut_kernel(split, src_ref, low_ref, high_ref, sems):
    copies = []
    for i, low in enumerate(range(0, src_ref.shape[0], CUT)):
        target = low_ref.at[pl.ds(low, CUT)] if low < split else high_ref.at[pl.ds(low - split, CUT)]
        copies.append(pltpu.make_async_copy(src_ref.at[pl.ds(low, CUT)], target, sems.at[i]))
    for copy in copies:
        copy.start()
    for copy in copies:
        copy.wait()


def cut(array, split):
    rows, width = array.shape
    return pl.pallas_call(
        functools.partial(cut_kernel, split),
        out_shape=[pltpu.VMEM((split, width), array.dtype), pltpu.VMEM((rows - split, width), array.dtype)],
        in_specs=[hbm_spec()],
        out_specs=[vmem_spec()] * 2,
        scratch_shapes=[pltpu.SemaphoreType.DMA((rows // CUT,))],
        compiler_params=pltpu.CompilerParams(vmem_limit_bytes=LIMIT),
        cost_estimate=SHORT,
        name="cut",
    )(in_hbm(array))


def join_kernel(a_ref, b_ref, out_ref):
    rows = a_ref.shape[0]
    out_ref[:rows, :] = a_ref[...]
    out_ref[rows:, :] = b_ref[...]


def middle_kernel(terms, shares, a_ref, total_ref, x_ref, w_ref, r_ref, cot_ref, *refs):
    last_ref, *refs = refs
    out_hbm, grad_ref, ax_ref, ht_ref, *share_refs, out_ref, sems = refs
    rows = x_ref.shape[0]
    step = rows // sems.shape[0]
    copies = []
    for i in range(sems.shape[0]):
        here = slice(i * step, (i + 1) * step)
        ax = total_ref[here, :]
        at = 0
        for part, low, high in terms:
            ax = ax + dot(a_ref[part, here, low:high], last_ref[at : at + high - low, :])
            at += high - low
        ax = ax.astype(BF16)
        ax_ref[here, :] = ax
        pre = dot(ax, w_ref[...]) + dot(x_ref[here, :], r_ref[...])
        gate = jax.nn.sigmoid(pre)
        out_ref[here, :] = (pre * gate).astype(BF16)
        copies.append(
            pltpu.make_async_copy(
                out_ref.at[pl.ds(i * step, step)], out_hbm.at[pl.ds(i * step, step)], sems.at[i]
            )
        )
        copies[-1].start()
        grad = (cot_ref[here, :].astype(F32) * (gate * (1.0 + pre * (1.0 - gate)))).astype(BF16)
        grad_ref[here, :] = grad
        ht_ref[:, here] = dot_nt(w_ref[...], grad).astype(BF16)
    for (part, low, high), share_ref in zip(shares, share_refs):
        share_ref[...] = dot(ht_ref[...], a_ref[part, :, low:high]).T.astype(BF16)
    for copy in copies:
        copy.wait()


def middle(terms, shares, *args):
    rows, width = args[2].shape
    wide = pltpu.VMEM((rows, width), BF16)
    return pl.pallas_call(
        functools.partial(middle_kernel, terms, shares),
        out_shape=[
            pltpu.HBM((rows, width), BF16), wide, wide, pltpu.VMEM((width, rows), BF16),
            *[pltpu.VMEM((high - low, width), BF16) for _, low, high in shares],
        ],
        in_specs=[vmem_spec()] * len(args),
        out_specs=[hbm_spec()] + [vmem_spec()] * (3 + len(shares)),
        scratch_shapes=[wide, pltpu.SemaphoreType.DMA((4,))],
        compiler_params=pltpu.CompilerParams(vmem_limit_bytes=LIMIT),
        cost_estimate=SHORT,
        name="middle",
    )(*[in_vmem(a) for a in args])


def spread_kernel(part, cuts, a_ref, ht_ref, *out_refs):
    for (low, high), out_ref in zip(cuts, out_refs):
        out_ref[...] = dot(ht_ref[...], a_ref[part, :, low:high]).T.astype(out_ref.dtype)


def spread(dense, ht, part, cuts, dtype, name):
    outs = [((high - low, ht.shape[0]), dtype) for low, high in cuts]
    return kernel_call(functools.partial(spread_kernel, part, cuts), name, outs, [dense, ht])


def pack_kernel(share_ref, other_ref, kept_ref, arrived_ref, out_ref):
    rows = share_ref.shape[0]
    out_ref[:rows, :] = (share_ref[...].astype(F32) + other_ref[...].astype(F32)).astype(BF16)
    out_ref[rows:, :] = (kept_ref[...] + arrived_ref[...]).astype(BF16)


def unpack_kernel(packed_ref, arrived_ref, share_ref, sum_ref):
    rows = share_ref.shape[0]
    share_ref[...] = arrived_ref[:rows, :]
    sum_ref[...] = (packed_ref[rows:, :].astype(F32) + arrived_ref[rows:, :].astype(F32)).astype(BF16)


def own_kernel(a_ref, ht_ref, grad_ref, r_ref, out_ref):
    half = out_ref.shape[0] // 2
    for here in (slice(0, half), slice(half, None)):
        out_ref[here, :] = dot(ht_ref[...], a_ref[OWN, :, here]).T + dot_nt(grad_ref[here, :], r_ref[...])


def final_kernel(split, own_ref, other_ref, low_ref, high_ref, direct_ref, out_ref):
    for rows, refs in ((slice(0, split), (low_ref,)), (slice(split, None), (high_ref, direct_ref))):
        total = own_ref[rows, :] + other_ref[rows, :].astype(F32)
        for ref in refs:
            total = total + ref[...].astype(F32)
        out_ref[rows, :] = total.astype(BF16)


def scaled_kernel(
    scale, out_ref, kept_ref, other_ref, out_hbm, weight_hbm, root_hbm, weight_ref, root_ref, sems
):
    copies = [pltpu.make_async_copy(out_ref, out_hbm, sems.at[0])]
    copies[0].start()
    core = lax.axis_index("row") & 1
    kept, other = kept_ref[...] * scale, other_ref[...] * scale
    weight_ref[...] = jnp.where(core == 0, kept, other)
    root_ref[...] = jnp.where(core == 0, other, kept)
    copies.append(pltpu.make_async_copy(weight_ref, weight_hbm, sems.at[1]))
    copies.append(pltpu.make_async_copy(root_ref, root_hbm, sems.at[2]))
    for copy in copies[1:]:
        copy.start()
    for copy in copies:
        copy.wait()


def scaled(scale, result, kept, other):
    shape = kept.shape
    return pl.pallas_call(
        functools.partial(scaled_kernel, scale),
        out_shape=[pltpu.HBM(result.shape, BF16), pltpu.HBM(shape, F32), pltpu.HBM(shape, F32)],
        in_specs=[vmem_spec()] * 3,
        out_specs=[hbm_spec()] * 3,
        scratch_shapes=[pltpu.VMEM(shape, F32)] * 2 + [pltpu.SemaphoreType.DMA((3,))],
        compiler_params=pltpu.CompilerParams(vmem_limit_bytes=LIMIT),
        cost_estimate=SHORT,
        name="scaled",
    )(in_vmem(result), in_vmem(kept), in_vmem(other))


def relay_kernel(own_ref, arrived_ref, out_ref):
    out_ref[...] = own_ref[...] + arrived_ref[...].astype(F32)


def relayed(own, arrived):
    return kernel_call(relay_kernel, "relay", [(own.shape, F32)], [own, arrived], RELAY)[0]


def weight_kernel(ax_ref, x_ref, grad_ref, kept_ref, sent_ref):
    core = lax.axis_index("row") & 1
    first = dot_tn(ax_ref[...], grad_ref[...])
    second = dot_tn(x_ref[...], grad_ref[...])
    kept_ref[...] = jnp.where(core == 0, first, second)
    sent_ref[...] = jnp.where(core == 0, second, first)


def exchanged(kept, hop, count):
    mine = kept.astype(BF16)
    return added(mine, lax.ppermute(mine, "row", [(i, i ^ hop) for i in range(count)]), F32)


def added(a, b, dtype=BF16):
    return (a.astype(F32) + b.astype(F32)).astype(dtype)


def body(features, weight, root_weight, block_tiles, tile_rows, tile_cols, tile_count, cotangent):
    count = lax.axis_size("row")
    rows, width = features.shape
    split = rows * FORWARD // 16

    low, high = cut(features, split)
    side_low = flip_side(low, count)
    passing = over_planes(high, count, True, "around")
    dense = dense_adjacency(tile_rows, tile_cols, tile_count, block_tiles, rows)
    whole, first, rest = (0, rows, 0), (0, split, 0), (split, rows, 0)
    own_x = flip_core(after(features, low), count)
    total = gathered(dense, [(OWN, *whole), (OWN_X, *whole)], [features, own_x], None, "gather_own")
    joined = kernel_call(join_kernel, "join", [((2 * (rows - split), width), BF16)], [high, after(passing, total, side_low)])[0]
    highs = flip_side(joined, count)
    side_low = after(side_low, joined)
    plane_low = over_planes(side_low, count, False, "around")
    side_x_low = flip_core(side_low, count)
    total = gathered(dense, [(SIDE, *first), (SIDE_X, *first)], [side_low, side_x_low], total, "gather_side")
    plane_low = after(plane_low, total)
    plane_x_low = flip_core(plane_low, count)
    highs_x = flip_core(highs, count)
    total = gathered(dense, [(SIDE, *rest), (PLANE, split, rows, rows - split)], [highs, highs], total, "gather_high")
    total = gathered(
        dense,
        [(PLANE, *first), (SIDE_X, *rest), (PLANE_X, split, rows, rows - split)],
        [plane_low, highs_x, highs_x],
        total,
        "gather_high_x",
        BRIEF,
    )

    split_back = rows * BACKWARD // 16
    back = [(0, split_back), (split_back, rows)]
    layer_out, grad_pre, gathered_x, ht, px_low, px_high, sx_high = middle(
        [(PLANE_X, 0, split)], [(PLANE_X, *back[0]), (PLANE_X, *back[1]), (SIDE_X, *back[1])],
        dense, total, features, weight, root_weight, cotangent, plane_x_low,
    )

    (p_low,) = spread(dense, ht, PLANE, back[:1], BF16, "spread_plane_low")
    p_low = added(p_low, flip_core(px_low, count))
    far = over_planes(p_low, count, True, "around")
    (p_high,) = spread(dense, after(ht, p_low), PLANE, back[1:], BF16, "spread_plane_high")

    square = ((width, width), F32)
    kept, sent = kernel_call(weight_kernel, "weight_products", [square, square], [gathered_x, features, grad_pre])
    high, wide = rows - split_back, (width, width)
    packed = kernel_call(
        pack_kernel, "pack", [((high + width, width), BF16)], [p_high, flip_core(px_high, count), kept, flip_core(sent, count)]
    )[0]
    passing, mine = kernel_call(
        unpack_kernel, "unpack", [((high, width), BF16), (wide, BF16)], [packed, flip_side(packed, count)]
    )

    (s_high,) = spread(dense, after(ht, packed), SIDE, back[1:], F32, "spread_side_high")
    s_high = added(s_high, flip_core(sx_high, count))
    near_high = flip_side(s_high, count)
    ht = after(ht, s_high)
    (sx_low,) = spread(dense, ht, SIDE_X, back[:1], BF16, "spread_side_x_low")
    sx_low = flip_core(sx_low, count)
    (s_low,) = spread(dense, after(ht, mine), SIDE, back[:1], F32, "spread_side_low")
    (ox,) = spread(dense, ht, OWN_X, [(0, rows)], BF16, "spread_own_x")
    own = kernel_call(own_kernel, "spread_own", [((rows, width), F32)], [dense, ht, grad_pre, root_weight])[0]
    through = added(relayed(after(s_low, own, ox, near_high), far), sx_low)
    near_low = flip_side(through, count)
    direct = over_planes(passing, count, False, None)
    theirs = lax.ppermute(after(mine, own), "row", [(i, i ^ 4) for i in range(count)])
    kept = added(mine, after(theirs, through), F32)
    hop = 8
    while hop < count:
        kept = exchanged(kept, hop, count)
        hop *= 2
    result = kernel_call(
        functools.partial(final_kernel, split_back), "final", [((rows, width), BF16)],
        [own, flip_core(ox, count), near_low, near_high, direct], LONG,
    )[0]
    grad_features, total_weight, total_root = scaled(
        1.0 / math.sqrt(count * rows), result, kept, flip_core(kept, count)
    )
    return layer_out, grad_features, total_weight, total_root


def solution(mesh):
    placed = (
        P(("groups", "row"), None),
        P(),
        P(),
        P(("groups", "row"), None, None),
        P(("groups", "row")),
        P(("groups", "row")),
        P(("groups", "row")),
        P(("groups", "row"), None),
    )
    return jax.shard_map(
        body,
        mesh=mesh,
        in_specs=placed,
        out_specs=(
            P(("groups", "row"), None),
            P(("groups", "row"), None),
            P("groups", None),
            P("groups", None),
        ),
        check_vma=False,
    )
```

```python
import functools
import math

import jax
import jax.numpy as jnp
from jax import lax
from jax.experimental import pallas as pl
from jax.experimental.pallas import tpu as pltpu
from jax.sharding import PartitionSpec as P

REACH = 2
F32, BF16 = jnp.float32, jnp.bfloat16

OWN, OWN_X, SIDE, SIDE_X, PLANE, PLANE_X = range(6)
PARTS = 6
LIMIT = 4 << 20
CUT = 64
SHORT = pl.CostEstimate(flops=0, bytes_accessed=0, transcendentals=0)
RELAY = pl.CostEstimate(flops=10**10, bytes_accessed=0, transcendentals=0)
BRIEF = pl.CostEstimate(flops=5 * 10**8, bytes_accessed=0, transcendentals=0)
LONG = pl.CostEstimate(flops=10**10, bytes_accessed=0, transcendentals=0)
FORWARD = 10
BACKWARD = 12


def vmem_spec():
    return pl.BlockSpec(memory_space=pltpu.VMEM)


def after(array, *others):
    return lax.optimization_barrier((array, *others))[0]


def smem_spec():
    return pl.BlockSpec(memory_space=pltpu.SMEM)


def hbm_spec():
    return pl.BlockSpec(memory_space=pltpu.HBM)


def in_vmem(array):
    return pltpu.with_memory_space_constraint(array, pltpu.VMEM)


def in_hbm(array):
    return pltpu.with_memory_space_constraint(array, pltpu.HBM)


def kernel_call(kernel, name, outs, args, cost=SHORT):
    return pl.pallas_call(
        kernel,
        out_shape=[pltpu.VMEM(shape, dtype) for shape, dtype in outs],
        in_specs=[vmem_spec()] * len(args),
        out_specs=[vmem_spec()] * len(outs),
        compiler_params=pltpu.CompilerParams(vmem_limit_bytes=LIMIT),
        cost_estimate=cost,
        name=name,
    )(*[in_vmem(a) for a in args])


def flip_core(array, count):
    return lax.ppermute(array, "row", [(i, i ^ 1) for i in range(count)])


def flip_side(array, count):
    return lax.ppermute(array, "row", [(i, i ^ 2) for i in range(count)])


def over_planes(array, count, back, ends):
    step = [(i, i + 4) for i in range(count) if i % 4 < 2 and i + 4 < count]
    step += [(i, i - 4) for i in range(count) if i % 4 >= 2 and i >= 4]
    if ends == "around":
        step += [(count - 4, 0), (count - 3, 1), (2, count - 2), (3, count - 1)]
    elif ends == "side":
        step += [(count - 4, count - 2), (count - 3, count - 1), (2, 0), (3, 1)]
    return lax.ppermute(array, "row", [(b, a) for a, b in step] if back else step)


def dense_kernel(count_ref, rows_hbm, cols_hbm, tiles_ref, a_ref, rows_ref, cols_ref, sem, index_sems):
    block = tiles_ref.shape[1]
    width = a_ref.shape[1]
    blocks = width // block
    fetches = [
        pltpu.make_async_copy(src, dst, index_sems.at[i])
        for i, (src, dst) in enumerate(((rows_hbm, rows_ref), (cols_hbm, cols_ref)))
    ]
    for fetch in fetches:
        fetch.start()
    stripe = lax.axis_index("row")
    core, side = stripe & 1, (stripe >> 1) & 1
    first = (stripe >> 1) * (2 * blocks)
    near = jnp.where(side == 0, 2, 0)

    def clear(i, carry):
        for part in range(PARTS):
            a_ref[part, pl.ds(pl.multiple_of(i * 64, 64), 64), :] = jnp.zeros((64, width), BF16)
        return carry

    def placed(slot):
        away = cols_ref[slot] - first + 2 * blocks
        stripe_at = lax.div(away, blocks) if blocks & (blocks - 1) else away >> (blocks.bit_length() - 1)
        column = away - stripe_at * blocks
        chip, other = stripe_at >> 1, stripe_at & 1
        part = jnp.where(chip == 1, OWN, jnp.where(chip == near, SIDE, PLANE)) + (other ^ core)
        target = a_ref.at[
            part,
            pl.ds(pl.multiple_of(rows_ref[slot] * block, block), block),
            pl.ds(pl.multiple_of(column * block, block), block),
        ]
        return pltpu.make_async_copy(tiles_ref.at[slot], target, sem)

    def start(slot, carry):
        placed(slot).start()
        return carry

    def start_four(group, carry):
        for i in range(4):
            placed(4 * group + i).start()
        return carry

    def finish(slot, carry):
        pltpu.make_async_copy(tiles_ref.at[0], a_ref.at[0, pl.ds(0, block), pl.ds(0, block)], sem).wait()
        return carry

    lax.fori_loop(0, width // 64, clear, 0)
    for fetch in fetches:
        fetch.wait()
    live = count_ref[0]
    lax.fori_loop(0, live >> 2, start_four, 0)
    lax.fori_loop((live >> 2) * 4, live, start, 0)
    lax.fori_loop(0, live, finish, 0)


def dense_adjacency(tile_rows, tile_cols, tile_count, block_tiles, width):
    slots = tile_rows.shape[0]
    return pl.pallas_call(
        dense_kernel,
        out_shape=pltpu.VMEM((PARTS, width, width), BF16),
        in_specs=[smem_spec()] + [hbm_spec()] * 3,
        out_specs=vmem_spec(),
        scratch_shapes=[
            pltpu.SMEM((slots,), jnp.int32),
            pltpu.SMEM((slots,), jnp.int32),
            pltpu.SemaphoreType.DMA,
            pltpu.SemaphoreType.DMA((2,)),
        ],
        compiler_params=pltpu.CompilerParams(vmem_limit_bytes=LIMIT),
        cost_estimate=SHORT,
        name="dense_adjacency",
    )(tile_count, *[in_hbm(a) for a in (tile_rows, tile_cols, block_tiles)])


def dot(a, b):
    return jnp.dot(a, b, preferred_element_type=F32)


def dot_nt(a, b):
    return lax.dot_general(a, b, (((1,), (1,)), ((), ())), preferred_element_type=F32)


def dot_tn(a, b):
    return lax.dot_general(a, b, (((0,), (0,)), ((), ())), preferred_element_type=F32)


def gather_kernel(terms, started, *refs):
    a_ref, out_ref = refs[0], refs[-1]
    sources = refs[1:-1]
    total = sources[-1][...] if started else None
    for (part, low, high, at), source in zip(terms, sources):
        product = dot(a_ref[part, :, low:high], source[at : at + high - low, :])
        total = product if total is None else total + product
    out_ref[...] = total


def gathered(dense, terms, sources, total, name, cost=SHORT):
    rows, width = dense.shape[1], sources[0].shape[1]
    args = [dense, *sources] + ([] if total is None else [total])
    return kernel_call(
        functools.partial(gather_kernel, terms, total is not None), name, [((rows, width), F32)], args, cost
    )[0]


def cut_kernel(split, src_ref, low_ref, high_ref, sems):
    copies = []
    for i, low in enumerate(range(0, src_ref.shape[0], CUT)):
        target = low_ref.at[pl.ds(low, CUT)] if low < split else high_ref.at[pl.ds(low - split, CUT)]
        copies.append(pltpu.make_async_copy(src_ref.at[pl.ds(low, CUT)], target, sems.at[i]))
    for copy in copies:
        copy.start()
    for copy in copies:
        copy.wait()


def cut(array, split):
    rows, width = array.shape
    return pl.pallas_call(
        functools.partial(cut_kernel, split),
        out_shape=[pltpu.VMEM((split, width), array.dtype), pltpu.VMEM((rows - split, width), array.dtype)],
        in_specs=[hbm_spec()],
        out_specs=[vmem_spec()] * 2,
        scratch_shapes=[pltpu.SemaphoreType.DMA((rows // CUT,))],
        compiler_params=pltpu.CompilerParams(vmem_limit_bytes=LIMIT),
        cost_estimate=SHORT,
        name="cut",
    )(in_hbm(array))


def join_kernel(a_ref, b_ref, out_ref):
    rows = a_ref.shape[0]
    out_ref[:rows, :] = a_ref[...]
    out_ref[rows:, :] = b_ref[...]


def middle_kernel(terms, shares, a_ref, total_ref, x_ref, w_ref, r_ref, cot_ref, *refs):
    last_ref, *refs = refs
    out_hbm, grad_ref, ax_ref, ht_ref, *share_refs, out_ref, sems = refs
    rows = x_ref.shape[0]
    step = rows // sems.shape[0]
    copies = []
    for i in range(sems.shape[0]):
        here = slice(i * step, (i + 1) * step)
        ax = total_ref[here, :]
        at = 0
        for part, low, high in terms:
            ax = ax + dot(a_ref[part, here, low:high], last_ref[at : at + high - low, :])
            at += high - low
        ax = ax.astype(BF16)
        ax_ref[here, :] = ax
        pre = dot(ax, w_ref[...]) + dot(x_ref[here, :], r_ref[...])
        gate = jax.nn.sigmoid(pre)
        out_ref[here, :] = (pre * gate).astype(BF16)
        copies.append(
            pltpu.make_async_copy(
                out_ref.at[pl.ds(i * step, step)], out_hbm.at[pl.ds(i * step, step)], sems.at[i]
            )
        )
        copies[-1].start()
        grad = (cot_ref[here, :].astype(F32) * (gate * (1.0 + pre * (1.0 - gate)))).astype(BF16)
        grad_ref[here, :] = grad
        ht_ref[:, here] = dot_nt(w_ref[...], grad).astype(BF16)
    for (part, low, high), share_ref in zip(shares, share_refs):
        share_ref[...] = dot(ht_ref[...], a_ref[part, :, low:high]).T.astype(BF16)
    for copy in copies:
        copy.wait()


def middle(terms, shares, *args):
    rows, width = args[2].shape
    wide = pltpu.VMEM((rows, width), BF16)
    return pl.pallas_call(
        functools.partial(middle_kernel, terms, shares),
        out_shape=[
            pltpu.HBM((rows, width), BF16), wide, wide, pltpu.VMEM((width, rows), BF16),
            *[pltpu.VMEM((high - low, width), BF16) for _, low, high in shares],
        ],
        in_specs=[vmem_spec()] * len(args),
        out_specs=[hbm_spec()] + [vmem_spec()] * (3 + len(shares)),
        scratch_shapes=[wide, pltpu.SemaphoreType.DMA((2,))],
        compiler_params=pltpu.CompilerParams(vmem_limit_bytes=LIMIT),
        cost_estimate=SHORT,
        name="middle",
    )(*[in_vmem(a) for a in args])


def spread_kernel(part, cuts, a_ref, ht_ref, *out_refs):
    for (low, high), out_ref in zip(cuts, out_refs):
        out_ref[...] = dot(ht_ref[...], a_ref[part, :, low:high]).T.astype(out_ref.dtype)


def spread(dense, ht, part, cuts, dtype, name):
    outs = [((high - low, ht.shape[0]), dtype) for low, high in cuts]
    return kernel_call(functools.partial(spread_kernel, part, cuts), name, outs, [dense, ht])


def pack_kernel(share_ref, other_ref, kept_ref, arrived_ref, out_ref):
    rows = share_ref.shape[0]
    out_ref[:rows, :] = (share_ref[...].astype(F32) + other_ref[...].astype(F32)).astype(BF16)
    out_ref[rows:, :] = (kept_ref[...] + arrived_ref[...]).astype(BF16)


def unpack_kernel(packed_ref, arrived_ref, share_ref, sum_ref):
    rows = share_ref.shape[0]
    share_ref[...] = arrived_ref[:rows, :]
    sum_ref[...] = (packed_ref[rows:, :].astype(F32) + arrived_ref[rows:, :].astype(F32)).astype(BF16)


def own_kernel(a_ref, ht_ref, grad_ref, r_ref, out_ref):
    half = out_ref.shape[0] // 2
    for here in (slice(0, half), slice(half, None)):
        out_ref[here, :] = dot(ht_ref[...], a_ref[OWN, :, here]).T + dot_nt(grad_ref[here, :], r_ref[...])


def final_kernel(split, own_ref, other_ref, low_ref, high_ref, direct_ref, out_ref):
    for rows, refs in ((slice(0, split), (low_ref,)), (slice(split, None), (high_ref, direct_ref))):
        total = own_ref[rows, :] + other_ref[rows, :].astype(F32)
        for ref in refs:
            total = total + ref[...].astype(F32)
        out_ref[rows, :] = total.astype(BF16)


def scaled_kernel(
    scale, out_ref, kept_ref, other_ref, out_hbm, weight_hbm, root_hbm, weight_ref, root_ref, sems
):
    copies = [pltpu.make_async_copy(out_ref, out_hbm, sems.at[0])]
    copies[0].start()
    core = lax.axis_index("row") & 1
    kept, other = kept_ref[...] * scale, other_ref[...] * scale
    weight_ref[...] = jnp.where(core == 0, kept, other)
    root_ref[...] = jnp.where(core == 0, other, kept)
    copies.append(pltpu.make_async_copy(weight_ref, weight_hbm, sems.at[1]))
    copies.append(pltpu.make_async_copy(root_ref, root_hbm, sems.at[2]))
    for copy in copies[1:]:
        copy.start()
    for copy in copies:
        copy.wait()


def scaled(scale, result, kept, other):
    shape = kept.shape
    return pl.pallas_call(
        functools.partial(scaled_kernel, scale),
        out_shape=[pltpu.HBM(result.shape, BF16), pltpu.HBM(shape, F32), pltpu.HBM(shape, F32)],
        in_specs=[vmem_spec()] * 3,
        out_specs=[hbm_spec()] * 3,
        scratch_shapes=[pltpu.VMEM(shape, F32)] * 2 + [pltpu.SemaphoreType.DMA((3,))],
        compiler_params=pltpu.CompilerParams(vmem_limit_bytes=LIMIT),
        cost_estimate=SHORT,
        name="scaled",
    )(in_vmem(result), in_vmem(kept), in_vmem(other))


def relay_kernel(own_ref, arrived_ref, out_ref):
    out_ref[...] = own_ref[...] + arrived_ref[...].astype(F32)


def relayed(own, arrived):
    return kernel_call(relay_kernel, "relay", [(own.shape, F32)], [own, arrived], RELAY)[0]


def weight_kernel(ax_ref, x_ref, grad_ref, kept_ref, sent_ref):
    core = lax.axis_index("row") & 1
    first = dot_tn(ax_ref[...], grad_ref[...])
    second = dot_tn(x_ref[...], grad_ref[...])
    kept_ref[...] = jnp.where(core == 0, first, second)
    sent_ref[...] = jnp.where(core == 0, second, first)


def exchanged(kept, hop, count):
    mine = kept.astype(BF16)
    return added(mine, lax.ppermute(mine, "row", [(i, i ^ hop) for i in range(count)]), F32)


def added(a, b, dtype=BF16):
    return (a.astype(F32) + b.astype(F32)).astype(dtype)


def body(features, weight, root_weight, block_tiles, tile_rows, tile_cols, tile_count, cotangent):
    count = lax.axis_size("row")
    rows, width = features.shape
    split = rows * FORWARD // 16

    low, high = cut(features, split)
    side_low = flip_side(low, count)
    passing = over_planes(high, count, True, "around")
    dense = dense_adjacency(tile_rows, tile_cols, tile_count, block_tiles, rows)
    whole, first, rest = (0, rows, 0), (0, split, 0), (split, rows, 0)
    own_x = flip_core(after(features, low), count)
    total = gathered(dense, [(OWN, *whole), (OWN_X, *whole)], [features, own_x], None, "gather_own")
    joined = kernel_call(join_kernel, "join", [((2 * (rows - split), width), BF16)], [high, after(passing, total, side_low)])[0]
    highs = flip_side(joined, count)
    side_low = after(side_low, joined)
    plane_low = over_planes(side_low, count, False, "around")
    side_x_low = flip_core(side_low, count)
    total = gathered(dense, [(SIDE, *first), (SIDE_X, *first)], [side_low, side_x_low], total, "gather_side")
    plane_low = after(plane_low, total)
    plane_x_low = flip_core(plane_low, count)
    highs_x = flip_core(after(highs, total), count)
    total = gathered(dense, [(SIDE, *rest), (PLANE, split, rows, rows - split)], [highs, highs], total, "gather_high")
    total = gathered(
        dense,
        [(PLANE, *first), (SIDE_X, *rest), (PLANE_X, split, rows, rows - split)],
        [plane_low, highs_x, highs_x],
        total,
        "gather_high_x",
        BRIEF,
    )

    split_back = rows * BACKWARD // 16
    back = [(0, split_back), (split_back, rows)]
    layer_out, grad_pre, gathered_x, ht, px_low, px_high, sx_high = middle(
        [(PLANE_X, 0, split)], [(PLANE_X, *back[0]), (PLANE_X, *back[1]), (SIDE_X, *back[1])],
        dense, total, features, weight, root_weight, cotangent, plane_x_low,
    )

    (p_low,) = spread(dense, ht, PLANE, back[:1], BF16, "spread_plane_low")
    p_low = added(p_low, flip_core(px_low, count))
    far = over_planes(p_low, count, True, "around")
    (p_high,) = spread(dense, after(ht, p_low), PLANE, back[1:], BF16, "spread_plane_high")

    square = ((width, width), F32)
    kept, sent = kernel_call(weight_kernel, "weight_products", [square, square], [gathered_x, features, grad_pre])
    high, wide = rows - split_back, (width, width)
    packed = kernel_call(
        pack_kernel, "pack", [((high + width, width), BF16)], [p_high, flip_core(px_high, count), kept, flip_core(sent, count)]
    )[0]
    passing, mine = kernel_call(
        unpack_kernel, "unpack", [((high, width), BF16), (wide, BF16)], [packed, flip_side(packed, count)]
    )

    ht = after(ht, packed)
    (ox,) = spread(dense, ht, OWN_X, [(0, rows)], BF16, "spread_own_x")
    own = kernel_call(own_kernel, "spread_own", [((rows, width), F32)], [dense, ht, grad_pre, root_weight])[0]
    ht = after(ht, own, ox)
    (s_high,) = spread(dense, ht, SIDE, back[1:], F32, "spread_side_high")
    s_high = added(s_high, flip_core(sx_high, count))
    near_high = flip_side(s_high, count)
    ht = after(ht, s_high)
    (sx_low,) = spread(dense, ht, SIDE_X, back[:1], BF16, "spread_side_x_low")
    sx_low = flip_core(sx_low, count)
    (s_low,) = spread(dense, after(ht, mine), SIDE, back[:1], F32, "spread_side_low")
    through = added(relayed(after(s_low, own, ox, near_high), far), sx_low)
    near_low = flip_side(through, count)
    direct = over_planes(passing, count, False, None)
    theirs = lax.ppermute(after(mine, own), "row", [(i, i ^ 4) for i in range(count)])
    kept = added(mine, after(theirs, through), F32)
    hop = 8
    while hop < count:
        kept = exchanged(kept, hop, count)
        hop *= 2
    result = kernel_call(
        functools.partial(final_kernel, split_back), "final", [((rows, width), BF16)],
        [own, flip_core(ox, count), near_low, near_high, direct], LONG,
    )[0]
    grad_features, total_weight, total_root = scaled(
        1.0 / math.sqrt(count * rows), result, kept, flip_core(kept, count)
    )
    return layer_out, grad_features, total_weight, total_root


def solution(mesh):
    placed = (
        P(("groups", "row"), None),
        P(),
        P(),
        P(("groups", "row"), None, None),
        P(("groups", "row")),
        P(("groups", "row")),
        P(("groups", "row")),
        P(("groups", "row"), None),
    )
    return jax.shard_map(
        body,
        mesh=mesh,
        in_specs=placed,
        out_specs=(
            P(("groups", "row"), None),
            P(("groups", "row"), None),
            P("groups", None),
            P("groups", None),
        ),
        check_vma=False,
    )
```

```python
import functools
import math

import jax
import jax.numpy as jnp
from jax import lax
from jax.experimental import pallas as pl
from jax.experimental.pallas import tpu as pltpu
from jax.sharding import PartitionSpec as P

REACH = 2
F32, BF16 = jnp.float32, jnp.bfloat16

OWN, OWN_X, SIDE, SIDE_X, PLANE, PLANE_X = range(6)
PARTS = 6
LIMIT = 4 << 20
CUT = 64
SHORT = pl.CostEstimate(flops=0, bytes_accessed=0, transcendentals=0)
RELAY = pl.CostEstimate(flops=10**10, bytes_accessed=0, transcendentals=0)
BRIEF = pl.CostEstimate(flops=5 * 10**8, bytes_accessed=0, transcendentals=0)
LONG = pl.CostEstimate(flops=10**10, bytes_accessed=0, transcendentals=0)
FORWARD = 10
BACKWARD = 12


def vmem_spec():
    return pl.BlockSpec(memory_space=pltpu.VMEM)


def after(array, *others):
    return lax.optimization_barrier((array, *others))[0]


def smem_spec():
    return pl.BlockSpec(memory_space=pltpu.SMEM)


def hbm_spec():
    return pl.BlockSpec(memory_space=pltpu.HBM)


def in_vmem(array):
    return pltpu.with_memory_space_constraint(array, pltpu.VMEM)


def in_hbm(array):
    return pltpu.with_memory_space_constraint(array, pltpu.HBM)


def kernel_call(kernel, name, outs, args, cost=SHORT):
    return pl.pallas_call(
        kernel,
        out_shape=[pltpu.VMEM(shape, dtype) for shape, dtype in outs],
        in_specs=[vmem_spec()] * len(args),
        out_specs=[vmem_spec()] * len(outs),
        compiler_params=pltpu.CompilerParams(vmem_limit_bytes=LIMIT),
        cost_estimate=cost,
        name=name,
    )(*[in_vmem(a) for a in args])


def flip_core(array, count):
    return lax.ppermute(array, "row", [(i, i ^ 1) for i in range(count)])


def flip_side(array, count):
    return lax.ppermute(array, "row", [(i, i ^ 2) for i in range(count)])


def over_planes(array, count, back, ends):
    step = [(i, i + 4) for i in range(count) if i % 4 < 2 and i + 4 < count]
    step += [(i, i - 4) for i in range(count) if i % 4 >= 2 and i >= 4]
    if ends == "around":
        step += [(count - 4, 0), (count - 3, 1), (2, count - 2), (3, count - 1)]
    elif ends == "side":
        step += [(count - 4, count - 2), (count - 3, count - 1), (2, 0), (3, 1)]
    return lax.ppermute(array, "row", [(b, a) for a, b in step] if back else step)


def dense_kernel(count_ref, rows_hbm, cols_hbm, tiles_ref, a_ref, rows_ref, cols_ref, sem, index_sems):
    block = tiles_ref.shape[1]
    width = a_ref.shape[1]
    blocks = width // block
    fetches = [
        pltpu.make_async_copy(src, dst, index_sems.at[i])
        for i, (src, dst) in enumerate(((rows_hbm, rows_ref), (cols_hbm, cols_ref)))
    ]
    for fetch in fetches:
        fetch.start()
    stripe = lax.axis_index("row")
    core, side = stripe & 1, (stripe >> 1) & 1
    first = (stripe >> 1) * (2 * blocks)
    near = jnp.where(side == 0, 2, 0)

    def clear(i, carry):
        for part in range(PARTS):
            a_ref[part, pl.ds(pl.multiple_of(i * 64, 64), 64), :] = jnp.zeros((64, width), BF16)
        return carry

    def placed(slot):
        away = cols_ref[slot] - first + 2 * blocks
        stripe_at = lax.div(away, blocks) if blocks & (blocks - 1) else away >> (blocks.bit_length() - 1)
        column = away - stripe_at * blocks
        chip, other = stripe_at >> 1, stripe_at & 1
        part = jnp.where(chip == 1, OWN, jnp.where(chip == near, SIDE, PLANE)) + (other ^ core)
        target = a_ref.at[
            part,
            pl.ds(pl.multiple_of(rows_ref[slot] * block, block), block),
            pl.ds(pl.multiple_of(column * block, block), block),
        ]
        return pltpu.make_async_copy(tiles_ref.at[slot], target, sem)

    def start(slot, carry):
        placed(slot).start()
        return carry

    def start_four(group, carry):
        for i in range(4):
            placed(4 * group + i).start()
        return carry

    def finish(slot, carry):
        pltpu.make_async_copy(tiles_ref.at[0], a_ref.at[0, pl.ds(0, block), pl.ds(0, block)], sem).wait()
        return carry

    lax.fori_loop(0, width // 64, clear, 0)
    for fetch in fetches:
        fetch.wait()
    live = count_ref[0]
    lax.fori_loop(0, live >> 2, start_four, 0)
    lax.fori_loop((live >> 2) * 4, live, start, 0)
    lax.fori_loop(0, live, finish, 0)


def dense_adjacency(tile_rows, tile_cols, tile_count, block_tiles, width):
    slots = tile_rows.shape[0]
    return pl.pallas_call(
        dense_kernel,
        out_shape=pltpu.VMEM((PARTS, width, width), BF16),
        in_specs=[smem_spec()] + [hbm_spec()] * 3,
        out_specs=vmem_spec(),
        scratch_shapes=[
            pltpu.SMEM((slots,), jnp.int32),
            pltpu.SMEM((slots,), jnp.int32),
            pltpu.SemaphoreType.DMA,
            pltpu.SemaphoreType.DMA((2,)),
        ],
        compiler_params=pltpu.CompilerParams(vmem_limit_bytes=LIMIT),
        cost_estimate=SHORT,
        name="dense_adjacency",
    )(tile_count, *[in_hbm(a) for a in (tile_rows, tile_cols, block_tiles)])


def dot(a, b):
    return jnp.dot(a, b, preferred_element_type=F32)


def dot_nt(a, b):
    return lax.dot_general(a, b, (((1,), (1,)), ((), ())), preferred_element_type=F32)


def dot_tn(a, b):
    return lax.dot_general(a, b, (((0,), (0,)), ((), ())), preferred_element_type=F32)


def gather_kernel(terms, started, *refs):
    a_ref, out_ref = refs[0], refs[-1]
    sources = refs[1:-1]
    total = sources[-1][...] if started else None
    for (part, low, high, at), source in zip(terms, sources):
        product = dot(a_ref[part, :, low:high], source[at : at + high - low, :])
        total = product if total is None else total + product
    out_ref[...] = total


def gathered(dense, terms, sources, total, name, cost=SHORT):
    rows, width = dense.shape[1], sources[0].shape[1]
    args = [dense, *sources] + ([] if total is None else [total])
    return kernel_call(
        functools.partial(gather_kernel, terms, total is not None), name, [((rows, width), F32)], args, cost
    )[0]


def cut_kernel(split, src_ref, low_ref, high_ref, sems):
    copies = []
    for i, low in enumerate(range(0, src_ref.shape[0], CUT)):
        target = low_ref.at[pl.ds(low, CUT)] if low < split else high_ref.at[pl.ds(low - split, CUT)]
        copies.append(pltpu.make_async_copy(src_ref.at[pl.ds(low, CUT)], target, sems.at[i]))
    for copy in copies:
        copy.start()
    for copy in copies:
        copy.wait()


def cut(array, split):
    rows, width = array.shape
    return pl.pallas_call(
        functools.partial(cut_kernel, split),
        out_shape=[pltpu.VMEM((split, width), array.dtype), pltpu.VMEM((rows - split, width), array.dtype)],
        in_specs=[hbm_spec()],
        out_specs=[vmem_spec()] * 2,
        scratch_shapes=[pltpu.SemaphoreType.DMA((rows // CUT,))],
        compiler_params=pltpu.CompilerParams(vmem_limit_bytes=LIMIT),
        cost_estimate=SHORT,
        name="cut",
    )(in_hbm(array))


def join_kernel(a_ref, b_ref, out_ref):
    rows = a_ref.shape[0]
    out_ref[:rows, :] = a_ref[...]
    out_ref[rows:, :] = b_ref[...]


def middle_kernel(terms, shares, a_ref, total_ref, x_ref, w_ref, r_ref, cot_ref, *refs):
    last_ref, *refs = refs
    out_ref, grad_ref, ax_ref, ht_ref, *share_refs = refs
    rows = x_ref.shape[0]
    step = rows // 2
    for i in range(2):
        here = slice(i * step, (i + 1) * step)
        ax = total_ref[here, :]
        at = 0
        for part, low, high in terms:
            ax = ax + dot(a_ref[part, here, low:high], last_ref[at : at + high - low, :])
            at += high - low
        ax = ax.astype(BF16)
        ax_ref[here, :] = ax
        pre = dot(ax, w_ref[...]) + dot(x_ref[here, :], r_ref[...])
        gate = jax.nn.sigmoid(pre)
        out_ref[here, :] = (pre * gate).astype(BF16)
        grad = (cot_ref[here, :].astype(F32) * (gate * (1.0 + pre * (1.0 - gate)))).astype(BF16)
        grad_ref[here, :] = grad
        ht_ref[:, here] = dot_nt(w_ref[...], grad).astype(BF16)
    for share, share_ref in zip(shares, share_refs):
        at = 0
        for part, low, high in share:
            share_ref[at : at + high - low, :] = dot(ht_ref[...], a_ref[part, :, low:high]).T.astype(BF16)
            at += high - low


def middle(terms, shares, *args):
    rows, width = args[2].shape
    wide = pltpu.VMEM((rows, width), BF16)
    return pl.pallas_call(
        functools.partial(middle_kernel, terms, shares),
        out_shape=[
            wide, wide, wide, pltpu.VMEM((width, rows), BF16),
            *[pltpu.VMEM((sum(high - low for _, low, high in share), width), BF16) for share in shares],
        ],
        in_specs=[vmem_spec()] * len(args),
        out_specs=[vmem_spec()] * (4 + len(shares)),
        compiler_params=pltpu.CompilerParams(vmem_limit_bytes=LIMIT),
        cost_estimate=SHORT,
        name="middle",
    )(*[in_vmem(a) for a in args])


def spread_kernel(part, cuts, a_ref, ht_ref, *out_refs):
    for (low, high), out_ref in zip(cuts, out_refs):
        out_ref[...] = dot(ht_ref[...], a_ref[part, :, low:high]).T.astype(out_ref.dtype)


def spread(dense, ht, part, cuts, dtype, name):
    outs = [((high - low, ht.shape[0]), dtype) for low, high in cuts]
    return kernel_call(functools.partial(spread_kernel, part, cuts), name, outs, [dense, ht])


def pack_kernel(share_ref, other_ref, kept_ref, arrived_ref, out_ref):
    rows = share_ref.shape[0]
    out_ref[:rows, :] = (share_ref[...].astype(F32) + other_ref[:rows, :].astype(F32)).astype(BF16)
    out_ref[rows:, :] = (kept_ref[...] + arrived_ref[...]).astype(BF16)


def unpack_kernel(packed_ref, arrived_ref, share_ref, sum_ref):
    rows = share_ref.shape[0]
    share_ref[...] = arrived_ref[:rows, :]
    sum_ref[...] = (packed_ref[rows:, :].astype(F32) + arrived_ref[rows:, :].astype(F32)).astype(BF16)


def own_kernel(a_ref, ht_ref, grad_ref, r_ref, done_ref, out_ref, done_hbm, sem):
    copy = pltpu.make_async_copy(done_ref, done_hbm, sem)
    copy.start()
    half = out_ref.shape[0] // 2
    for here in (slice(0, half), slice(half, None)):
        out_ref[here, :] = dot(ht_ref[...], a_ref[OWN, :, here]).T + dot_nt(grad_ref[here, :], r_ref[...])
    copy.wait()


def own_share(*args):
    shape = args[-1].shape
    return pl.pallas_call(
        own_kernel,
        out_shape=[pltpu.VMEM(shape, F32), pltpu.HBM(shape, BF16)],
        in_specs=[vmem_spec()] * len(args),
        out_specs=[vmem_spec(), hbm_spec()],
        scratch_shapes=[pltpu.SemaphoreType.DMA],
        compiler_params=pltpu.CompilerParams(vmem_limit_bytes=LIMIT),
        cost_estimate=SHORT,
        name="spread_own",
    )(*[in_vmem(a) for a in args])


def final_kernel(split, own_ref, other_ref, low_ref, high_ref, direct_ref, out_ref):
    for rows, refs in ((slice(0, split), (low_ref,)), (slice(split, None), (high_ref, direct_ref))):
        total = own_ref[rows, :] + other_ref[rows, :].astype(F32)
        for ref in refs:
            total = total + ref[...].astype(F32)
        out_ref[rows, :] = total.astype(BF16)


def scaled_kernel(
    scale, out_ref, kept_ref, other_ref, out_hbm, weight_hbm, root_hbm, weight_ref, root_ref, sems
):
    copies = [pltpu.make_async_copy(out_ref, out_hbm, sems.at[0])]
    copies[0].start()
    core = lax.axis_index("row") & 1
    kept, other = kept_ref[...] * scale, other_ref[...] * scale
    weight_ref[...] = jnp.where(core == 0, kept, other)
    root_ref[...] = jnp.where(core == 0, other, kept)
    copies.append(pltpu.make_async_copy(weight_ref, weight_hbm, sems.at[1]))
    copies.append(pltpu.make_async_copy(root_ref, root_hbm, sems.at[2]))
    for copy in copies[1:]:
        copy.start()
    for copy in copies:
        copy.wait()


def scaled(scale, result, kept, other):
    shape = kept.shape
    return pl.pallas_call(
        functools.partial(scaled_kernel, scale),
        out_shape=[pltpu.HBM(result.shape, BF16), pltpu.HBM(shape, F32), pltpu.HBM(shape, F32)],
        in_specs=[vmem_spec()] * 3,
        out_specs=[hbm_spec()] * 3,
        scratch_shapes=[pltpu.VMEM(shape, F32)] * 2 + [pltpu.SemaphoreType.DMA((3,))],
        compiler_params=pltpu.CompilerParams(vmem_limit_bytes=LIMIT),
        cost_estimate=SHORT,
        name="scaled",
    )(in_vmem(result), in_vmem(kept), in_vmem(other))


def relay_kernel(own_ref, arrived_ref, out_ref):
    out_ref[...] = own_ref[...] + arrived_ref[...].astype(F32)


def relayed(own, arrived):
    return kernel_call(relay_kernel, "relay", [(own.shape, F32)], [own, arrived], RELAY)[0]


def weight_kernel(ax_ref, x_ref, grad_ref, kept_ref, sent_ref):
    core = lax.axis_index("row") & 1
    first = dot_tn(ax_ref[...], grad_ref[...])
    second = dot_tn(x_ref[...], grad_ref[...])
    kept_ref[...] = jnp.where(core == 0, first, second)
    sent_ref[...] = jnp.where(core == 0, second, first)


def exchanged(kept, hop, count):
    mine = kept.astype(BF16)
    return added(mine, lax.ppermute(mine, "row", [(i, i ^ hop) for i in range(count)]), F32)


def added(a, b, dtype=BF16):
    return (a.astype(F32) + b.astype(F32)).astype(dtype)


def body(features, weight, root_weight, block_tiles, tile_rows, tile_cols, tile_count, cotangent):
    count = lax.axis_size("row")
    rows, width = features.shape
    split = rows * FORWARD // 16

    low, high = cut(features, split)
    side_low = flip_side(low, count)
    passing = over_planes(high, count, True, "around")
    dense = dense_adjacency(tile_rows, tile_cols, tile_count, block_tiles, rows)
    whole, first, rest = (0, rows, 0), (0, split, 0), (split, rows, 0)
    own_x = flip_core(after(features, low), count)
    total = gathered(dense, [(OWN, *whole), (OWN_X, *whole)], [features, own_x], None, "gather_own")
    joined = kernel_call(join_kernel, "join", [((2 * (rows - split), width), BF16)], [high, after(passing, total, side_low)])[0]
    highs = flip_side(joined, count)
    side_low = after(side_low, joined)
    plane_low = over_planes(side_low, count, False, "around")
    side_x_low = flip_core(side_low, count)
    total = gathered(dense, [(SIDE, *first), (SIDE_X, *first)], [side_low, side_x_low], total, "gather_side")
    highs_x = flip_core(after(highs, total), count)
    total = gathered(dense, [(SIDE, *rest), (PLANE, split, rows, rows - split)], [highs, highs], total, "gather_high")
    plane_low = after(plane_low, total)
    plane_x_low = flip_core(plane_low, count)
    total = gathered(
        dense,
        [(PLANE, *first), (SIDE_X, *rest), (PLANE_X, split, rows, rows - split)],
        [plane_low, highs_x, highs_x],
        total,
        "gather_high_x",
        BRIEF,
    )

    split_back = rows * BACKWARD // 16
    back = [(0, split_back), (split_back, rows)]
    layer_out, grad_pre, gathered_x, ht, px_low, x_high = middle(
        [(PLANE_X, 0, split)], [[(PLANE_X, *back[0])], [(PLANE_X, *back[1]), (SIDE_X, *back[1])]],
        dense, total, features, weight, root_weight, cotangent, plane_x_low,
    )

    (p_low,) = spread(dense, ht, PLANE, back[:1], BF16, "spread_plane_low")
    p_low = added(p_low, flip_core(px_low, count))
    far = over_planes(p_low, count, True, "around")
    (p_high,) = spread(dense, after(ht, p_low), PLANE, back[1:], BF16, "spread_plane_high")
    x_high = flip_core(x_high, count)

    square = ((width, width), F32)
    kept, sent = kernel_call(weight_kernel, "weight_products", [square, square], [gathered_x, features, grad_pre])
    high, wide = rows - split_back, (width, width)
    packed = kernel_call(
        pack_kernel, "pack", [((high + width, width), BF16)], [p_high, x_high, kept, flip_core(sent, count)]
    )[0]
    passing, mine = kernel_call(
        unpack_kernel, "unpack", [((high, width), BF16), (wide, BF16)], [packed, flip_side(packed, count)]
    )

    ht = after(ht, packed)
    (ox,) = spread(dense, ht, OWN_X, [(0, rows)], BF16, "spread_own_x")
    own, layer_out = own_share(dense, ht, grad_pre, root_weight, layer_out)
    ht = after(ht, own, ox)
    (s_high,) = spread(dense, ht, SIDE, back[1:], F32, "spread_side_high")
    s_high = added(s_high, x_high[high:])
    near_high = flip_side(s_high, count)
    ht = after(ht, s_high)
    (sx_low,) = spread(dense, ht, SIDE_X, back[:1], BF16, "spread_side_x_low")
    sx_low = flip_core(sx_low, count)
    (s_low,) = spread(dense, after(ht, mine), SIDE, back[:1], F32, "spread_side_low")
    through = added(relayed(after(s_low, own, ox, near_high), far), sx_low)
    near_low = flip_side(through, count)
    direct = over_planes(passing, count, False, None)
    theirs = lax.ppermute(after(mine, own), "row", [(i, i ^ 4) for i in range(count)])
    kept = added(mine, after(theirs, through), F32)
    hop = 8
    while hop < count:
        kept = exchanged(kept, hop, count)
        hop *= 2
    result = kernel_call(
        functools.partial(final_kernel, split_back), "final", [((rows, width), BF16)],
        [own, flip_core(ox, count), near_low, near_high, direct], LONG,
    )[0]
    grad_features, total_weight, total_root = scaled(
        1.0 / math.sqrt(count * rows), result, kept, flip_core(kept, count)
    )
    return layer_out, grad_features, total_weight, total_root


def solution(mesh):
    placed = (
        P(("groups", "row"), None),
        P(),
        P(),
        P(("groups", "row"), None, None),
        P(("groups", "row")),
        P(("groups", "row")),
        P(("groups", "row")),
        P(("groups", "row"), None),
    )
    return jax.shard_map(
        body,
        mesh=mesh,
        in_specs=placed,
        out_specs=(
            P(("groups", "row"), None),
            P(("groups", "row"), None),
            P("groups", None),
            P("groups", None),
        ),
        check_vma=False,
    )
```
